256 devices in a mesh: seq: 64 (over z, y, core), book: 4 (over x).
Axes of the slice: x: 4, y: 4, z: 8, core: 2. Of those that a mesh axis runs over, the one named last changes fastest.
Arguments:
- frames: bfloat16 [65536, 1024], P('seq'), may hold values from -6 to 6
- norm_gain: float32 [1024], replicated, may hold values from 0.5 to 1.5
- x_weight: bfloat16 [1024, 2048], P(None, 'book'), may hold values from -0.1875 to 0.1875
- z_weight: bfloat16 [1024, 2048], P(None, 'book'), may hold values from -0.1875 to 0.1875
- bc_weight: bfloat16 [1024, 256], replicated, may hold values from -0.1875 to 0.1875
- dt_weight: bfloat16 [1024, 16], P(None, 'book'), may hold values from -0.1875 to 0.1875
- dt_bias: float32 [16], P('book'), may hold values from -1.5 to 0.5
- decay_rate: float32 [16], P('book'), may hold values from 7.6293945e-07 to 0.1
- out_gain: float32 [2048], P('book'), may hold values from 0.5 to 1.5
- out_weight: bfloat16 [2048, 1024], P('book'), may hold values from -0.125 to 0.125
- codebook: float32 [3, 65536, 1024], P(None, 'seq', 'book'), may hold values from -4 to 4
- code_ids: int32 [3, 16384], P(None, 'seq'), may hold values from 0 to 65535, as said below
Outputs:
- residual: float32 [16384, 1024], P('seq', 'book')
- code_grad: float32 [3, 65536, 1024], P(None, 'seq', 'book')
The draws below stay inside these ranges and needn't reach their ends.
Inputs may be any that keep to these rules, and one draw needn't show every extreme that they name: `code_ids`: the owner of a code is its index // 1024. In each level, of the 256 rows of one seq index at most 12 name codes of one owner; one owner, drawn for each level and different in different levels, gets exactly 12 rows from every seq index; every other owner gets at most 4. The owner that gets 12 rows in level 0 gets exactly 4 rows from every seq index in every other level, so that over all levels the rows of one seq index name codes of one owner at most 20 times, and exactly so for that owner.
All inputs are finite; a program needn't handle non-finite values.
Results may differ from the reference program's by a relative error of at most 0.005.
Values sent between devices are 32-bit elements; how exact they have to be, the bound alone decides.
No kernel may reach another device: no remote copies, remote signals or barrier semaphores. Data moves between devices by JAX's collectives and lax.ppermute only.
A program may use at most 128 MiB of HBM per device.

```python
import math
import jax
import jax.numpy as jnp
from jax import lax

D = 1024
HEADS = 16
HEAD_DIM = 128
STATE = 128
CODES = 65536
BLOCK = 256
POOL = 4
LEVELS = 3
INNER = 2048
FRAMES = 65536
QROWS_DEV = 256
QROWS = 16384
CODES_OWN = 1024
LOW = 4
CAP = 12
N_SEQ = 64


def draw_code_ids(key, part):
    base_key = jax.random.fold_in(key, 3)
    hottest_all = jax.random.permutation(jax.random.fold_in(base_key, 1), N_SEQ)[:LEVELS].astype(jnp.int32)
    level_range = jnp.arange(LEVELS, dtype=jnp.int32)
    second_all = jnp.where(level_range == 0, hottest_all[1], hottest_all[0])

    def one_level(level_idx):
        level_key = jax.random.fold_in(base_key, level_idx + 100)
        hottest = hottest_all[level_idx]
        second = second_all[level_idx]
        lower_owner = jnp.minimum(hottest, second)
        upper_owner = jnp.maximum(hottest, second)

        def one_device(device_idx):
            device_key = jax.random.fold_in(level_key, device_idx + 11)
            first_key, second_key, third_key = jax.random.split(device_key, 3)
            spread = jax.random.permutation(first_key, (N_SEQ - 2) * LOW)[:QROWS_DEV - CAP - LOW]
            others = (spread // LOW).astype(jnp.int32)
            others = others + (others >= lower_owner).astype(jnp.int32)
            others = others + (others >= upper_owner).astype(jnp.int32)
            owner_list = jnp.concatenate([jnp.full((CAP,), hottest, jnp.int32), jnp.full((LOW,), second, jnp.int32), others])
            owner_list = jax.random.permutation(second_key, owner_list)
            local_rows = jax.random.randint(third_key, (QROWS_DEV,), 0, CODES_OWN)
            return owner_list * CODES_OWN + local_rows
        return jax.vmap(one_device)(jnp.arange(N_SEQ, dtype=jnp.int32)).reshape(-1)
    return jax.vmap(one_level)(level_range).astype(jnp.int32)


def draw_decay_rate(key, part):
    first_key, second_key, third_key = jax.random.split(jax.random.fold_in(key, 5), 3)
    share = 0.5
    slow_heads = jax.random.uniform(first_key, (HEADS,)) < share
    slow_rates = jnp.exp(jax.random.uniform(second_key, (HEADS,), minval=math.log(0.05 / FRAMES), maxval=math.log(1.0 / FRAMES)))
    fast_rates = jnp.exp(jax.random.uniform(third_key, (HEADS,), minval=math.log(0.02), maxval=math.log(0.1)))
    return jnp.where(slow_heads, slow_rates, fast_rates).astype(jnp.float32)


def levels(key, extent, cuts, smallest, high):
    def one(position, blocks):
        heights = jax.random.uniform(jax.random.fold_in(jax.random.fold_in(key, 6), position), (blocks,), jnp.float32, smallest / len(cuts), high / len(cuts))
        return jnp.repeat(jnp.exp(heights), extent[position] // blocks).reshape((-1,) + (1,) * (len(extent) - position - 1))

    gain = one(*cuts[0])
    for cut in cuts[1:]:
        gain = gain * one(*cut)
    return gain


def normal_values(key, extent, deviation, reach, cuts=(), kind=jnp.bfloat16):
    drawn = deviation * jax.random.normal(key, extent, jnp.float32)
    if cuts:
        drawn = drawn * levels(key, extent, cuts, -0.22, 0.18)
    return jnp.clip(drawn, -reach, reach).astype(kind)


def setup_inputs(seed: int = 0) -> dict:
    splits = jax.random.split(jax.random.key(seed), 13)
    frames = normal_values(splits[0], (FRAMES, D), 1.0, 6.0, ((0, 64),))
    norm_gain = jnp.clip(1.0 + 0.1 * jax.random.normal(splits[1], (D,), jnp.float32), 0.5, 1.5)
    x_weight = normal_values(splits[2], (D, INNER), D ** -0.5, 0.1875, ((1, 4),))
    z_weight = normal_values(splits[3], (D, INNER), D ** -0.5, 0.1875, ((1, 4),))
    bc_weight = normal_values(splits[4], (D, 2 * STATE), D ** -0.5, 0.1875)
    dt_weight = normal_values(splits[5], (D, HEADS), D ** -0.5, 0.1875, ((1, 4),))
    dt_bias = jnp.clip(-1.5 + 2.0 * jax.random.uniform(splits[6], (HEADS,), jnp.float32) ** levels(splits[6], (HEADS,), ((0, 4),), -0.2, 0.2), -1.5, 0.5)
    decay_rate = draw_decay_rate(jax.random.fold_in(splits[12], 71), 0)
    out_gain = jnp.clip(1.0 + 0.1 * jax.random.normal(splits[8], (INNER,), jnp.float32), 0.5, 1.5)
    out_weight = normal_values(splits[9], (INNER, D), INNER ** -0.5, 0.125, ((0, 4),))
    codebook = normal_values(splits[10], (LEVELS, CODES, D), 0.5, 4.0, ((1, 64), (2, 4)), jnp.float32)
    code_ids = draw_code_ids(jax.random.fold_in(splits[12], 71), 0)
    return dict(frames=frames, norm_gain=norm_gain, x_weight=x_weight, z_weight=z_weight, bc_weight=bc_weight, dt_weight=dt_weight, dt_bias=dt_bias, decay_rate=decay_rate, out_gain=out_gain, out_weight=out_weight, codebook=codebook, code_ids=code_ids)


def rms_scaled(values, scales):
    mean_square = lax.optimization_barrier(jnp.mean(values * values, axis=-1, keepdims=True))
    return values * lax.rsqrt(mean_square + 1e-05) * scales

def block_pass(carried, inputs):
    x_part, b_part, c_part, dt_part, log_part = inputs
    cumulative = jnp.cumsum(log_part, axis=0)
    length = log_part.shape[0]
    causal = jnp.arange(length)[:, None] >= jnp.arange(length)[None, :]
    log_gaps = cumulative[:, None, :] - cumulative[None, :, :]
    weights = jnp.where(causal[:, :, None], jnp.exp(jnp.where(causal[:, :, None], log_gaps, 0.0)), 0.0)
    scores = jnp.dot(c_part, b_part.T, precision=lax.Precision.HIGHEST)
    inflow = x_part * dt_part[:, :, None]
    outputs = jnp.einsum('tjh,jhp->thp', weights * scores[:, :, None], inflow, precision=lax.Precision.HIGHEST)
    outputs = outputs + jnp.exp(cumulative)[:, :, None] * jnp.einsum('tn,hpn->thp', c_part, carried, precision=lax.Precision.HIGHEST)
    tail_decay = jnp.exp(cumulative[-1:] - cumulative)
    updated = jnp.exp(cumulative[-1])[:, None, None] * carried + jnp.einsum('jh,jhp,jn->hpn', tail_decay, inflow, b_part, precision=lax.Precision.HIGHEST)
    return (updated, outputs)

def reference(frames, norm_gain, x_weight, z_weight, bc_weight, dt_weight, dt_bias, decay_rate, out_gain, out_weight, codebook, code_ids):
    frames_wide = frames.astype(jnp.float32)
    normed = rms_scaled(frames_wide, norm_gain).astype(jnp.bfloat16)
    x_proj = jnp.dot(normed, x_weight, preferred_element_type=jnp.float32).astype(jnp.bfloat16)
    z_proj = jnp.dot(normed, z_weight, preferred_element_type=jnp.float32).astype(jnp.bfloat16)
    bc_proj = jnp.dot(normed, bc_weight, preferred_element_type=jnp.float32).astype(jnp.bfloat16)
    dt_full = jax.nn.softplus(jnp.dot(normed, dt_weight, preferred_element_type=jnp.float32) + dt_bias)
    x_act = jax.nn.silu(x_proj.astype(jnp.float32)).reshape(FRAMES, HEADS, HEAD_DIM)
    bc_act = jax.nn.silu(bc_proj.astype(jnp.float32))
    b_full = bc_act[:, :STATE]
    c_full = bc_act[:, STATE:]
    log_decay = -dt_full * decay_rate
    blocks = FRAMES // BLOCK
    stacked = (x_act.reshape(blocks, BLOCK, HEADS, HEAD_DIM), b_full.reshape(blocks, BLOCK, STATE), c_full.reshape(blocks, BLOCK, STATE), dt_full.reshape(blocks, BLOCK, HEADS), log_decay.reshape(blocks, BLOCK, HEADS))
    initial = jnp.zeros((HEADS, HEAD_DIM, STATE), jnp.float32)
    ssd_out = lax.scan(block_pass, initial, stacked)[1]
    ssd_out = ssd_out.reshape(FRAMES, HEADS, HEAD_DIM)
    gated_rows = ssd_out * jax.nn.silu(z_proj.astype(jnp.float32)).reshape(FRAMES, HEADS, HEAD_DIM)
    gated_rows = rms_scaled(gated_rows, out_gain.reshape(HEADS, HEAD_DIM)).reshape(FRAMES, INNER).astype(jnp.bfloat16)
    encoded = frames_wide + jnp.dot(gated_rows, out_weight, preferred_element_type=jnp.float32)
    pooled = lax.optimization_barrier(jnp.mean(encoded.reshape(QROWS, POOL, D), axis=1))
    residual = pooled
    gradients = []
    for level_idx in range(LEVELS):
        picked = codebook[level_idx][code_ids[level_idx]]
        gradients.append(jnp.zeros((CODES, D), jnp.float32).at[code_ids[level_idx]].add(picked - residual))
        residual = residual - picked
    return (residual, jnp.stack(gradients))
```

```python
import jax
import jax.numpy as jnp
from jax import lax
from jax.experimental import pallas as pl
from jax.experimental.pallas import tpu as pltpu
from jax.sharding import Mesh
from jax.sharding import PartitionSpec as P

SEQ = ("seq_0", "seq_1", "seq_2")
OWNERS = 64
SLOTS = 20
TOTAL = OWNERS * SLOTS
LEVELS = 3
CODES = 1024
FRAMES = 1024
BLOCK = 256
STEPS = FRAMES // BLOCK
QROWS = 256
WIDTH = 256
HEADS = 4
DIM = 128
INNER = HEADS * DIM
PAYLOAD = 10 * 128

f32 = jnp.float32
bf16 = jnp.bfloat16
HIGHEST = lax.Precision.HIGHEST
NT = (((1,), (1,)), ((), ()))


def dot(a, b):
    return jnp.dot(a, b, preferred_element_type=f32)


def dot_exact(a, b):
    return jnp.dot(a, b, preferred_element_type=f32, precision=HIGHEST)


def iota(shape, dim):
    return lax.broadcasted_iota(jnp.int32, shape, dim)


def two_parts(values):
    high = values.astype(bf16)
    low = (values - high.astype(f32)).astype(bf16)
    return jnp.concatenate([high, low], axis=1)


def folded(values):
    half = values.shape[1] // 2
    return values[:, :half] + values[:, half:]


def silu(values):
    return values * jax.nn.sigmoid(values)


def per_head(columns):
    rows = columns.shape[0]
    return jnp.concatenate(
        [jnp.broadcast_to(columns[:, h : h + 1], (rows, DIM)) for h in range(HEADS)], axis=1
    )


def causal_f32():
    return (iota((BLOCK, BLOCK), 0) >= iota((BLOCK, BLOCK), 1)).astype(f32)


def state_step(state, decayed, cum, b_act):
    return state * per_head(jnp.exp(cum[BLOCK - 1 :, :])) + dot(b_act.T, decayed)


def place_codes(ids_ref, slots_ref):
    entries = LEVELS * QROWS
    ids = jnp.concatenate([ids_ref[k : k + 1, :] for k in range(LEVELS)], axis=1)
    level = iota((1, entries), 1) // QROWS
    owner = ids // CODES
    wanted = level * CODES + ids % CODES + 1
    member = (iota((OWNERS, entries), 0) == owner).astype(f32)
    before = (iota((entries, entries), 0) < iota((entries, entries), 1)).astype(bf16)
    rank = jnp.sum(member * dot(member.astype(bf16), before), axis=0, keepdims=True)
    rank = rank.astype(jnp.int32)
    slot = owner * SLOTS + rank
    for k in range(LEVELS):
        slots_ref[k : k + 1, :] = slot[:, k * QROWS : (k + 1) * QROWS]
    ranked = (iota((128, entries), 0) == rank).astype(bf16)
    high = (member * (wanted // 64).astype(f32)).astype(bf16)
    low = (member * (wanted % 64).astype(f32)).astype(bf16)
    return 64.0 * lax.dot_general(high, ranked, NT, preferred_element_type=f32) + lax.dot_general(
        low, ranked, NT, preferred_element_type=f32
    )


def front_kernel(
    frames_ref, gain_ref, x_w_ref, bc_w_ref, dt_w_ref, bias_ref, rate_ref, ids_ref,
    payload_ref, slots_ref, normed_ref, inflow_ref, bc_ref, log_ref,
    state_ref, total_ref,
):
    step = pl.program_id(0)

    @pl.when(step == 0)
    def _():
        state_ref[...] = jnp.zeros_like(state_ref)
        total_ref[...] = jnp.zeros_like(total_ref)
        asked = place_codes(ids_ref, slots_ref)
        for k in range(OWNERS):
            payload_ref[k, :, 1152:1280] = asked[k : k + 1, :]

    frames = frames_ref[...].astype(f32)
    square = jnp.mean(frames * frames, axis=1, keepdims=True)
    normed = (frames * lax.rsqrt(square + 1e-05) * gain_ref[...]).astype(bf16)
    normed_ref[...] = normed
    bc_act = silu(dot(normed, bc_w_ref[...]).astype(bf16).astype(f32)).astype(bf16)
    bc_ref[...] = bc_act
    raw = dot(normed, dt_w_ref[...]) + bias_ref[...]
    dt = jnp.maximum(raw, 0.0) + jnp.log1p(jnp.exp(-jnp.abs(raw)))
    log = -dt * rate_ref[...]
    log_ref[...] = log
    cum = dot_exact(causal_f32(), log)
    x_act = silu(dot(normed, x_w_ref[...]).astype(bf16).astype(f32))
    inflow = x_act * per_head(dt)
    inflow_ref[...] = inflow.astype(bf16)
    last = cum[BLOCK - 1 :, :]
    decayed = (inflow * per_head(jnp.exp(last - cum))).astype(bf16)
    state_ref[...] = state_step(state_ref[...], decayed, cum, bc_act[:, :DIM])
    total_ref[0:1, 0:HEADS] += last

    @pl.when(step == STEPS - 1)
    def _():
        for k in range(OWNERS):
            head, row = k // 16, (k % 16) * 8
            lanes = slice(head * DIM, (head + 1) * DIM)
            for r in range(8):
                payload_ref[k, :, r * 128 : (r + 1) * 128] = state_ref[row + r : row + r + 1, lanes]
            payload_ref[k, :, 1024:1152] = jnp.broadcast_to(
                total_ref[0:1, head : head + 1], (1, 128)
            )


def scan_kernel(arrived_ref, before_ref):
    carried = [jnp.zeros((1, 128), f32) for _ in range(8)]
    for k in range(OWNERS):
        decay = jnp.exp(arrived_ref[k, :, 1024:1152])
        for r in range(8):
            before_ref[k, r : r + 1, :] = carried[r]
            carried[r] = carried[r] * decay + arrived_ref[k, :, r * 128 : (r + 1) * 128]


def local_kernel(
    frames_ref, normed_ref, inflow_ref, bc_ref, log_ref, z_w_ref,
    inner_ref, gate_ref, reach_ref, means_ref,
    state_ref, total_ref,
):
    @pl.when(pl.program_id(0) == 0)
    def _():
        state_ref[...] = jnp.zeros_like(state_ref)
        total_ref[...] = jnp.zeros_like(total_ref)

    gate_ref[...] = silu(dot(normed_ref[...], z_w_ref[...]).astype(bf16).astype(f32))
    pool = jnp.where(
        iota((BLOCK // 4, BLOCK), 0) == iota((BLOCK // 4, BLOCK), 1) // 4, 0.25, 0.0
    ).astype(bf16)
    means = dot(pool, frames_ref[...])
    for g in range(4):
        means_ref[g] = means[:, g * WIDTH : (g + 1) * WIDTH]
    causal = iota((BLOCK, BLOCK), 0) >= iota((BLOCK, BLOCK), 1)
    log = log_ref[...]
    cum = dot_exact(causal.astype(f32), log)
    cum_rows = lax.dot_general(
        jnp.concatenate([log, jnp.zeros((BLOCK, 128 - HEADS), f32)], axis=1).T,
        causal.astype(f32), NT, preferred_element_type=f32, precision=HIGHEST,
    )
    b_act, c_act = bc_ref[:, :DIM], bc_ref[:, DIM:]
    inflow = inflow_ref[...]
    scores = jnp.where(causal, lax.dot_general(c_act, b_act, NT, preferred_element_type=f32), 0.0)
    carried = dot(c_act, state_ref[...].astype(bf16)) * per_head(jnp.exp(cum))
    for h in range(HEADS):
        lanes = slice(h * DIM, (h + 1) * DIM)
        gaps = jnp.minimum(cum[:, h : h + 1] - cum_rows[h : h + 1, :], 0.0)
        mixed = (jnp.exp(gaps) * scores).astype(bf16)
        inner_ref[:, lanes] = dot(mixed, inflow[:, lanes]) + carried[:, lanes]
    reach_ref[...] = jnp.exp(cum + total_ref[0:1, 0:HEADS])
    last = cum[BLOCK - 1 :, :]
    total_ref[0:1, 0:HEADS] += last
    decayed = (inflow.astype(f32) * per_head(jnp.exp(last - cum))).astype(bf16)
    state_ref[...] = state_step(state_ref[...], decayed, cum, b_act)


def outer_kernel(
    book_ref, inner_ref, gate_ref, reach_ref, c_ref, incoming_ref, gain_ref, out_w_ref,
    out_0, out_1, out_2, out_3, pooled_ref,
):
    step = pl.program_id(0)
    pool = jnp.where(
        iota((BLOCK // 4, BLOCK), 0) == iota((BLOCK // 4, BLOCK), 1) // 4, 0.25, 0.0
    ).astype(bf16)
    c_act = c_ref[...]
    for h in range(HEADS):
        lanes = slice(h * DIM, (h + 1) * DIM)
        carried = dot(c_act, incoming_ref[lanes, :].astype(bf16))
        rows = (inner_ref[:, lanes] + carried * reach_ref[:, h : h + 1]) * gate_ref[:, lanes]
        square = jnp.mean(rows * rows, axis=1, keepdims=True)
        rows = (rows * lax.rsqrt(square + 1e-05) * gain_ref[:, lanes]).astype(bf16)
        pooled_ref[pl.ds(step * (BLOCK // 4), BLOCK // 4), lanes] = dot(pool, rows)

    @pl.when(step == STEPS - 1)
    def _():
        pooled = pooled_ref[...]
        high = pooled.astype(bf16)
        low = (pooled - high.astype(f32)).astype(bf16)
        both = jnp.concatenate([high, low], axis=0)
        for shift, out in enumerate((out_0, out_1, out_2, out_3)):
            start = pl.multiple_of(((book_ref[0] + shift) % 4) * WIDTH, WIDTH)
            product = dot(both, out_w_ref[:, pl.ds(start, WIDTH)])
            out[...] = product[:QROWS] + product[QROWS:]


def lookup_kernel(codes_ref, table_ref, found_ref, parts_ref):
    @pl.when(pl.program_id(0) == 0)
    def _():
        parts_ref[...] = two_parts(table_ref[...])

    rows = codes_ref.shape[0]
    chosen = (codes_ref[...] == iota((rows, LEVELS * CODES), 1) + 1).astype(bf16)
    found = folded(dot(chosen, parts_ref[...]))
    found_ref[pl.ds(0, rows, 2), :] = found[:, :128]
    found_ref[pl.ds(1, rows, 2), :] = found[:, 128:]


def joined_rows(ref):
    half = ref.shape[0] // 2
    return jnp.concatenate([ref[pl.ds(0, half, 2), :], ref[pl.ds(1, half, 2), :]], axis=1)


def taken_kernel(found_ref, slots_ref, terms_ref, taken_ref):
    found = joined_rows(found_ref)
    parts = two_parts(found)
    slots = jnp.concatenate(
        [slots_ref[...].astype(f32), jnp.zeros((8 - LEVELS, QROWS), f32)], axis=0
    )
    same = (iota((QROWS, QROWS), 0) == iota((QROWS, QROWS), 1)).astype(f32)
    columns = lax.dot_general(same, slots, NT, preferred_element_type=f32, precision=HIGHEST)
    columns = columns.astype(jnp.int32)
    taken = jnp.zeros((QROWS, WIDTH), f32)
    terms = found
    for k in range(LEVELS):
        if k:
            spread = (iota((TOTAL, QROWS), 0) == slots_ref[k : k + 1, :]).astype(bf16)
            terms = terms + folded(dot(spread, two_parts(taken)))
        picks = (columns[:, k : k + 1] == iota((QROWS, TOTAL), 1)).astype(bf16)
        taken = taken + folded(dot(picks, parts))
    terms_ref[...] = terms
    taken_ref[...] = taken


def residual_kernel(
    book_ref, own_ref, from_1, from_2, from_3, means_ref, taken_ref, terms_ref, slots_ref,
    residual_ref, grads_ref,
):
    pooled = own_ref[...] + from_1[...] + from_2[...] + from_3[...] + means_ref[0]
    residual_ref[...] = pooled - taken_ref[...]
    place = iota((TOTAL, QROWS), 0)
    spread = place == slots_ref[0:1, :]
    for k in range(1, LEVELS):
        spread = spread | (place == slots_ref[k : k + 1, :])
    grads = terms_ref[...] - folded(dot(spread.astype(bf16), two_parts(pooled)))
    grads_ref[pl.ds(0, TOTAL, 2), :] = grads[:, :128]
    grads_ref[pl.ds(1, TOTAL, 2), :] = grads[:, 128:]


def table_kernel(codes_ref, grads_ref, table_ref, parts_ref):
    step = pl.program_id(0)

    @pl.when(step == 0)
    def _():
        parts_ref[...] = two_parts(joined_rows(grads_ref))

    rows = table_ref.shape[0]
    chosen = (codes_ref[...] == iota((rows, TOTAL), 0) + (step * rows + 1)).astype(bf16)
    table_ref[...] = folded(dot(chosen, parts_ref[...]))


def shape(*dims, dtype=f32):
    return jax.ShapeDtypeStruct(dims, dtype)


def whole(*dims):
    return pl.BlockSpec(dims, lambda *_: (0,) * len(dims))


def rows_of(rows, columns):
    return pl.BlockSpec((rows, columns), lambda i, *_: (i, 0))


def settings(mib):
    return pltpu.CompilerParams(vmem_limit_bytes=mib * 2**20)


def exchange(array):
    return lax.all_to_all(array, SEQ, split_axis=0, concat_axis=0, tiled=True)


def body(
    frames, norm_gain, x_weight, z_weight, bc_weight, dt_weight, dt_bias, decay_rate,
    out_gain, out_weight, codebook, code_ids,
):
    book = lax.axis_index("book").reshape(1)
    payload, slots, normed, inflow, bc_act, log = pl.pallas_call(
        front_kernel,
        grid=(STEPS,),
        in_specs=[
            rows_of(BLOCK, 1024), whole(1, 1024), whole(1024, INNER), whole(1024, 256),
            whole(1024, HEADS), whole(1, HEADS), whole(1, HEADS), whole(LEVELS, QROWS),
        ],
        out_specs=[
            whole(OWNERS, 1, PAYLOAD), whole(LEVELS, QROWS), rows_of(BLOCK, 1024),
            rows_of(BLOCK, INNER), rows_of(BLOCK, 256), rows_of(BLOCK, HEADS),
        ],
        out_shape=[
            shape(OWNERS, 1, PAYLOAD), shape(LEVELS, QROWS, dtype=jnp.int32),
            shape(FRAMES, 1024, dtype=bf16), shape(FRAMES, INNER, dtype=bf16),
            shape(FRAMES, 256, dtype=bf16), shape(FRAMES, HEADS),
        ],
        scratch_shapes=[pltpu.VMEM((DIM, INNER), f32), pltpu.VMEM((8, 128), f32)],
        compiler_params=settings(32),
        name="front",
    )(
        frames, norm_gain.reshape(1, -1), x_weight, bc_weight, dt_weight,
        dt_bias.reshape(1, -1), decay_rate.reshape(1, -1), code_ids,
    )
    arrived = exchange(payload)
    inner, gate, reach, means = pl.pallas_call(
        local_kernel,
        grid=(STEPS,),
        in_specs=[
            rows_of(BLOCK, 1024), rows_of(BLOCK, 1024), rows_of(BLOCK, INNER),
            rows_of(BLOCK, 256), rows_of(BLOCK, HEADS), whole(1024, INNER),
        ],
        out_specs=[
            rows_of(BLOCK, INNER), rows_of(BLOCK, INNER), rows_of(BLOCK, HEADS),
            pl.BlockSpec((4, BLOCK // 4, WIDTH), lambda i: (0, i, 0)),
        ],
        out_shape=[
            shape(FRAMES, INNER), shape(FRAMES, INNER), shape(FRAMES, HEADS),
            shape(4, QROWS, WIDTH),
        ],
        scratch_shapes=[pltpu.VMEM((DIM, INNER), f32), pltpu.VMEM((8, 128), f32)],
        compiler_params=settings(32),
        cost_estimate=pl.CostEstimate(flops=4 * 10**9, bytes_accessed=12 * 2**20, transcendentals=10**6),
        name="local",
    )(frames, normed, inflow, bc_act, log, z_weight)
    before = pl.pallas_call(
        scan_kernel,
        out_shape=shape(OWNERS, 8, 128),
        name="scan",
    )(arrived)
    incoming = exchange(before).reshape(INNER, DIM)
    asked = arrived[:, 0, 1152 : 1152 + SLOTS].astype(jnp.int32)
    codes_column = asked.reshape(TOTAL, 1)
    codes_row = asked.reshape(1, TOTAL)
    found = pl.pallas_call(
        lookup_kernel,
        grid=(5,),
        in_specs=[rows_of(TOTAL // 5, 1), whole(LEVELS * CODES, WIDTH)],
        out_specs=rows_of(2 * TOTAL // 5, 128),
        out_shape=shape(2 * TOTAL, 128),
        scratch_shapes=[pltpu.VMEM((LEVELS * CODES, 2 * WIDTH), bf16)],
        compiler_params=settings(32),
        cost_estimate=pl.CostEstimate(flops=6 * 10**9, bytes_accessed=5 * 2**20, transcendentals=0),
        name="lookup",
    )(codes_column, codebook.reshape(LEVELS * CODES, WIDTH))
    fetched = exchange(found.reshape(OWNERS, 2 * SLOTS, 128)).reshape(2 * TOTAL, 128)
    shares = pl.pallas_call(
        outer_kernel,
        grid_spec=pltpu.PrefetchScalarGridSpec(
            num_scalar_prefetch=1,
            grid=(STEPS,),
            in_specs=[
                rows_of(BLOCK, INNER), rows_of(BLOCK, INNER), rows_of(BLOCK, HEADS),
                pl.BlockSpec((BLOCK, DIM), lambda i, *_: (i, 1)),
                whole(INNER, DIM), whole(1, INNER), whole(INNER, 1024),
            ],
            out_specs=[whole(QROWS, WIDTH)] * 4,
            scratch_shapes=[pltpu.VMEM((QROWS, INNER), f32)],
        ),
        out_shape=[shape(QROWS, WIDTH)] * 4,
        compiler_params=settings(32),
        cost_estimate=pl.CostEstimate(flops=2 * 10**9, bytes_accessed=8 * 2**20, transcendentals=10**5),
        name="outer",
    )(book, inner, gate, reach, bc_act, incoming, out_gain.reshape(1, -1), out_weight)
    moved = [
        lax.ppermute(shares[d], "book", [(i, (i + d) % 4) for i in range(4)]) for d in (1, 2, 3)
    ]
    terms, taken = pl.pallas_call(
        taken_kernel,
        out_shape=[shape(TOTAL, WIDTH), shape(QROWS, WIDTH)],
        compiler_params=settings(48),
        cost_estimate=pl.CostEstimate(flops=3 * 10**9, bytes_accessed=3 * 2**20, transcendentals=0),
        name="taken",
    )(fetched, slots)
    residual, grads = pl.pallas_call(
        residual_kernel,
        grid_spec=pltpu.PrefetchScalarGridSpec(
            num_scalar_prefetch=1,
            grid=(1,),
            in_specs=[whole(QROWS, WIDTH)] * 4
            + [
                pl.BlockSpec((1, QROWS, WIDTH), lambda i, book: (book[0], 0, 0)),
                whole(QROWS, WIDTH), whole(TOTAL, WIDTH), whole(LEVELS, QROWS),
            ],
            out_specs=[whole(QROWS, WIDTH), whole(2 * TOTAL, 128)],
        ),
        out_shape=[shape(QROWS, WIDTH), shape(2 * TOTAL, 128)],
        compiler_params=settings(48),
        name="residual",
    )(book, shares[0], *moved, means, taken, terms, slots)
    returned = exchange(grads.reshape(OWNERS, 2 * SLOTS, 128)).reshape(2 * TOTAL, 128)
    table = pl.pallas_call(
        table_kernel,
        grid=(6,),
        in_specs=[whole(1, TOTAL), whole(2 * TOTAL, 128)],
        out_specs=rows_of(LEVELS * CODES // 6, WIDTH),
        out_shape=shape(LEVELS * CODES, WIDTH),
        scratch_shapes=[pltpu.VMEM((TOTAL, 2 * WIDTH), bf16)],
        compiler_params=settings(32),
        name="table",
    )(codes_row, returned)
    return residual, table.reshape(LEVELS, CODES, WIDTH)


def solution(mesh):
    finer = Mesh(
        mesh.devices.reshape(8, 4, 2, mesh.shape["book"]), ("seq_0", "seq_1", "seq_2", "book")
    )
    placed = (
        P(SEQ, None), P(), P(None, "book"), P(None, "book"), P(), P(None, "book"), P("book"),
        P("book"), P("book"), P("book", None), P(None, SEQ, "book"), P(None, SEQ),
    )
    return jax.shard_map(
        body,
        mesh=finer,
        in_specs=placed,
        out_specs=(P(SEQ, "book"), P(None, SEQ, "book")),
        check_vma=False,
    )
```

```python
import jax
import jax.numpy as jnp
from jax import lax
from jax.experimental import pallas as pl
from jax.experimental.pallas import tpu as pltpu
from jax.sharding import Mesh
from jax.sharding import PartitionSpec as P

SEQ = ("seq_0", "seq_1", "seq_2")
OWNERS = 64
SLOTS = 20
TOTAL = OWNERS * SLOTS
LEVELS = 3
CODES = 1024
FRAMES = 1024
BLOCK = 256
STEPS = FRAMES // BLOCK
QROWS = 256
WIDTH = 256
HEADS = 4
DIM = 128
INNER = HEADS * DIM
PAYLOAD = 10 * 128

f32 = jnp.float32
bf16 = jnp.bfloat16
HIGHEST = lax.Precision.HIGHEST
NT = (((1,), (1,)), ((), ()))


def dot(a, b):
    return jnp.dot(a, b, preferred_element_type=f32)


def dot_exact(a, b):
    return jnp.dot(a, b, preferred_element_type=f32, precision=HIGHEST)


def iota(shape, dim):
    return lax.broadcasted_iota(jnp.int32, shape, dim)


def two_parts(values):
    high = values.astype(bf16)
    low = (values - high.astype(f32)).astype(bf16)
    return jnp.concatenate([high, low], axis=1)


def folded(values):
    half = values.shape[1] // 2
    return values[:, :half] + values[:, half:]


def silu(values):
    return values * jax.nn.sigmoid(values)


def per_head(columns):
    rows = columns.shape[0]
    return jnp.concatenate(
        [jnp.broadcast_to(columns[:, h : h + 1], (rows, DIM)) for h in range(HEADS)], axis=1
    )


def causal_f32():
    return (iota((BLOCK, BLOCK), 0) >= iota((BLOCK, BLOCK), 1)).astype(f32)


def state_step(state, decayed, cum, b_act):
    return state * per_head(jnp.exp(cum[BLOCK - 1 :, :])) + dot(b_act.T, decayed)


def place_codes(ids_ref, slots_ref):
    entries = LEVELS * QROWS
    ids = jnp.concatenate([ids_ref[k : k + 1, :] for k in range(LEVELS)], axis=1)
    level = iota((1, entries), 1) // QROWS
    owner = ids // CODES
    wanted = level * CODES + ids % CODES + 1
    member = (iota((OWNERS, entries), 0) == owner).astype(f32)
    before = (iota((entries, entries), 0) < iota((entries, entries), 1)).astype(bf16)
    rank = jnp.sum(member * dot(member.astype(bf16), before), axis=0, keepdims=True)
    rank = rank.astype(jnp.int32)
    slot = owner * SLOTS + rank
    for k in range(LEVELS):
        slots_ref[k : k + 1, :] = slot[:, k * QROWS : (k + 1) * QROWS]
    ranked = (iota((128, entries), 0) == rank).astype(bf16)
    high = (member * (wanted // 64).astype(f32)).astype(bf16)
    low = (member * (wanted % 64).astype(f32)).astype(bf16)
    return 64.0 * lax.dot_general(high, ranked, NT, preferred_element_type=f32) + lax.dot_general(
        low, ranked, NT, preferred_element_type=f32
    )


def front_kernel(
    frames_ref, gain_ref, x_w_ref, bc_w_ref, dt_w_ref, bias_ref, rate_ref, ids_ref,
    payload_ref, slots_ref, normed_ref, inflow_ref, bc_ref, log_ref,
    state_ref, total_ref,
):
    step = pl.program_id(0)

    @pl.when(step == 0)
    def _():
        state_ref[...] = jnp.zeros_like(state_ref)
        total_ref[...] = jnp.zeros_like(total_ref)
        asked = place_codes(ids_ref, slots_ref)
        for k in range(OWNERS):
            payload_ref[k, :, 1152:1280] = asked[k : k + 1, :]

    frames = frames_ref[...].astype(f32)
    square = jnp.mean(frames * frames, axis=1, keepdims=True)
    normed = (frames * lax.rsqrt(square + 1e-05) * gain_ref[...]).astype(bf16)
    normed_ref[...] = normed
    bc_act = silu(dot(normed, bc_w_ref[...]).astype(bf16).astype(f32)).astype(bf16)
    bc_ref[...] = bc_act
    raw = dot(normed, dt_w_ref[...]) + bias_ref[...]
    dt = jnp.maximum(raw, 0.0) + jnp.log1p(jnp.exp(-jnp.abs(raw)))
    log = -dt * rate_ref[...]
    log_ref[...] = log
    cum = dot_exact(causal_f32(), log)
    x_act = silu(dot(normed, x_w_ref[...]).astype(bf16).astype(f32))
    inflow = x_act * per_head(dt)
    inflow_ref[...] = inflow.astype(bf16)
    last = cum[BLOCK - 1 :, :]
    decayed = (inflow * per_head(jnp.exp(last - cum))).astype(bf16)
    state_ref[...] = state_step(state_ref[...], decayed, cum, bc_act[:, :DIM])
    total_ref[0:1, 0:HEADS] += last

    @pl.when(step == STEPS - 1)
    def _():
        for k in range(OWNERS):
            head, row = k // 16, (k % 16) * 8
            lanes = slice(head * DIM, (head + 1) * DIM)
            for r in range(8):
                payload_ref[k, :, r * 128 : (r + 1) * 128] = state_ref[row + r : row + r + 1, lanes]
            payload_ref[k, :, 1024:1152] = jnp.broadcast_to(
                total_ref[0:1, head : head + 1], (1, 128)
            )


def scan_kernel(arrived_ref, before_ref):
    carried = [jnp.zeros((1, 128), f32) for _ in range(8)]
    for k in range(OWNERS):
        decay = jnp.exp(arrived_ref[k, :, 1024:1152])
        for r in range(8):
            before_ref[k, r : r + 1, :] = carried[r]
            carried[r] = carried[r] * decay + arrived_ref[k, :, r * 128 : (r + 1) * 128]


def local_kernel(
    frames_ref, normed_ref, inflow_ref, bc_ref, log_ref, z_w_ref,
    inner_ref, gate_ref, reach_ref, means_ref,
    state_ref, total_ref,
):
    @pl.when(pl.program_id(0) == 0)
    def _():
        state_ref[...] = jnp.zeros_like(state_ref)
        total_ref[...] = jnp.zeros_like(total_ref)

    gate_ref[...] = silu(dot(normed_ref[...], z_w_ref[...]).astype(bf16).astype(f32))
    pool = jnp.where(
        iota((BLOCK // 4, BLOCK), 0) == iota((BLOCK // 4, BLOCK), 1) // 4, 0.25, 0.0
    ).astype(bf16)
    means = dot(pool, frames_ref[...])
    for g in range(4):
        means_ref[g] = means[:, g * WIDTH : (g + 1) * WIDTH]
    causal = iota((BLOCK, BLOCK), 0) >= iota((BLOCK, BLOCK), 1)
    log = log_ref[...]
    cum = dot_exact(causal.astype(f32), log)
    cum_rows = lax.dot_general(
        jnp.concatenate([log, jnp.zeros((BLOCK, 128 - HEADS), f32)], axis=1).T,
        causal.astype(f32), NT, preferred_element_type=f32, precision=HIGHEST,
    )
    b_act, c_act = bc_ref[:, :DIM], bc_ref[:, DIM:]
    inflow = inflow_ref[...]
    scores = jnp.where(causal, lax.dot_general(c_act, b_act, NT, preferred_element_type=f32), 0.0)
    carried = dot(c_act, state_ref[...].astype(bf16)) * per_head(jnp.exp(cum))
    for h in range(HEADS):
        lanes = slice(h * DIM, (h + 1) * DIM)
        gaps = jnp.minimum(cum[:, h : h + 1] - cum_rows[h : h + 1, :], 0.0)
        mixed = (jnp.exp(gaps) * scores).astype(bf16)
        inner_ref[:, lanes] = dot(mixed, inflow[:, lanes]) + carried[:, lanes]
    reach_ref[...] = jnp.exp(cum + total_ref[0:1, 0:HEADS])
    last = cum[BLOCK - 1 :, :]
    total_ref[0:1, 0:HEADS] += last
    decayed = (inflow.astype(f32) * per_head(jnp.exp(last - cum))).astype(bf16)
    state_ref[...] = state_step(state_ref[...], decayed, cum, b_act)


def outer_kernel(
    book_ref, inner_ref, gate_ref, reach_ref, c_ref, incoming_ref, gain_ref, out_w_ref,
    out_0, out_1, out_2, out_3, pooled_ref,
):
    step = pl.program_id(0)
    pool = jnp.where(
        iota((BLOCK // 4, BLOCK), 0) == iota((BLOCK // 4, BLOCK), 1) // 4, 0.25, 0.0
    ).astype(bf16)
    c_act = c_ref[...]
    for h in range(HEADS):
        lanes = slice(h * DIM, (h + 1) * DIM)
        carried = dot(c_act, incoming_ref[lanes, :].astype(bf16))
        rows = (inner_ref[:, lanes] + carried * reach_ref[:, h : h + 1]) * gate_ref[:, lanes]
        square = jnp.mean(rows * rows, axis=1, keepdims=True)
        rows = (rows * lax.rsqrt(square + 1e-05) * gain_ref[:, lanes]).astype(bf16)
        pooled_ref[pl.ds(step * (BLOCK // 4), BLOCK // 4), lanes] = dot(pool, rows)

    @pl.when(step == STEPS - 1)
    def _():
        pooled = pooled_ref[...]
        high = pooled.astype(bf16)
        low = (pooled - high.astype(f32)).astype(bf16)
        both = jnp.concatenate([high, low], axis=0)
        for shift, out in enumerate((out_0, out_1, out_2, out_3)):
            start = pl.multiple_of(((book_ref[0] + shift) % 4) * WIDTH, WIDTH)
            product = dot(both, out_w_ref[:, pl.ds(start, WIDTH)])
            out[...] = product[:QROWS] + product[QROWS:]


def lookup_kernel(codes_ref, table_ref, found_ref, parts_ref):
    @pl.when(pl.program_id(0) == 0)
    def _():
        parts_ref[...] = two_parts(table_ref[...])

    rows = codes_ref.shape[0]
    chosen = (codes_ref[...] == iota((rows, LEVELS * CODES), 1) + 1).astype(bf16)
    found = folded(dot(chosen, parts_ref[...]))
    found_ref[pl.ds(0, rows, 2), :] = found[:, :128]
    found_ref[pl.ds(1, rows, 2), :] = found[:, 128:]


def joined_rows(ref):
    half = ref.shape[0] // 2
    return jnp.concatenate([ref[pl.ds(0, half, 2), :], ref[pl.ds(1, half, 2), :]], axis=1)


def taken_kernel(found_ref, slots_ref, terms_ref, taken_ref):
    found = joined_rows(found_ref)
    parts = two_parts(found)
    slots = jnp.concatenate(
        [slots_ref[...].astype(f32), jnp.zeros((8 - LEVELS, QROWS), f32)], axis=0
    )
    same = (iota((QROWS, QROWS), 0) == iota((QROWS, QROWS), 1)).astype(f32)
    columns = lax.dot_general(same, slots, NT, preferred_element_type=f32, precision=HIGHEST)
    columns = columns.astype(jnp.int32)
    taken = jnp.zeros((QROWS, WIDTH), f32)
    terms = found
    for k in range(LEVELS):
        if k:
            spread = (iota((TOTAL, QROWS), 0) == slots_ref[k : k + 1, :]).astype(bf16)
            terms = terms + folded(dot(spread, two_parts(taken)))
        picks = (columns[:, k : k + 1] == iota((QROWS, TOTAL), 1)).astype(bf16)
        taken = taken + folded(dot(picks, parts))
    terms_ref[...] = terms
    taken_ref[...] = taken


def residual_kernel(
    book_ref, own_ref, from_1, from_2, from_3, means_ref, taken_ref, terms_ref, slots_ref,
    residual_ref, grads_ref,
):
    pooled = own_ref[...] + from_1[...] + from_2[...] + from_3[...] + means_ref[0]
    residual_ref[...] = pooled - taken_ref[...]
    place = iota((TOTAL, QROWS), 0)
    spread = place == slots_ref[0:1, :]
    for k in range(1, LEVELS):
        spread = spread | (place == slots_ref[k : k + 1, :])
    grads = terms_ref[...] - folded(dot(spread.astype(bf16), two_parts(pooled)))
    grads_ref[pl.ds(0, TOTAL, 2), :] = grads[:, :128]
    grads_ref[pl.ds(1, TOTAL, 2), :] = grads[:, 128:]


def table_kernel(codes_ref, grads_ref, table_ref, parts_ref):
    step = pl.program_id(0)

    @pl.when(step == 0)
    def _():
        parts_ref[...] = two_parts(joined_rows(grads_ref))

    rows = table_ref.shape[0]
    chosen = (codes_ref[...] == iota((rows, TOTAL), 0) + (step * rows + 1)).astype(bf16)
    table_ref[...] = folded(dot(chosen, parts_ref[...]))


def shape(*dims, dtype=f32):
    return jax.ShapeDtypeStruct(dims, dtype)


def whole(*dims):
    return pl.BlockSpec(dims, lambda *_: (0,) * len(dims))


def rows_of(rows, columns):
    return pl.BlockSpec((rows, columns), lambda i, *_: (i, 0))


def settings(mib):
    return pltpu.CompilerParams(vmem_limit_bytes=mib * 2**20)


def exchange(array):
    return lax.all_to_all(array, SEQ, split_axis=0, concat_axis=0, tiled=True)


def body(
    frames, norm_gain, x_weight, z_weight, bc_weight, dt_weight, dt_bias, decay_rate,
    out_gain, out_weight, codebook, code_ids,
):
    book = lax.axis_index("book").reshape(1)
    payload, slots, normed, inflow, bc_act, log = pl.pallas_call(
        front_kernel,
        grid=(STEPS,),
        in_specs=[
            rows_of(BLOCK, 1024), whole(1, 1024), whole(1024, INNER), whole(1024, 256),
            whole(1024, HEADS), whole(1, HEADS), whole(1, HEADS), whole(LEVELS, QROWS),
        ],
        out_specs=[
            whole(OWNERS, 1, PAYLOAD), whole(LEVELS, QROWS), rows_of(BLOCK, 1024),
            rows_of(BLOCK, INNER), rows_of(BLOCK, 256), rows_of(BLOCK, HEADS),
        ],
        out_shape=[
            shape(OWNERS, 1, PAYLOAD), shape(LEVELS, QROWS, dtype=jnp.int32),
            shape(FRAMES, 1024, dtype=bf16), shape(FRAMES, INNER, dtype=bf16),
            shape(FRAMES, 256, dtype=bf16), shape(FRAMES, HEADS),
        ],
        scratch_shapes=[pltpu.VMEM((DIM, INNER), f32), pltpu.VMEM((8, 128), f32)],
        compiler_params=settings(62),
        name="front",
    )(
        frames, norm_gain.reshape(1, -1), x_weight, bc_weight, dt_weight,
        dt_bias.reshape(1, -1), decay_rate.reshape(1, -1), code_ids,
    )
    arrived = exchange(payload)
    inner, gate, reach, means = pl.pallas_call(
        local_kernel,
        grid=(STEPS,),
        in_specs=[
            rows_of(BLOCK, 1024), rows_of(BLOCK, 1024), rows_of(BLOCK, INNER),
            rows_of(BLOCK, 256), rows_of(BLOCK, HEADS), whole(1024, INNER),
        ],
        out_specs=[
            rows_of(BLOCK, INNER), rows_of(BLOCK, INNER), rows_of(BLOCK, HEADS),
            pl.BlockSpec((4, BLOCK // 4, WIDTH), lambda i: (0, i, 0)),
        ],
        out_shape=[
            shape(FRAMES, INNER), shape(FRAMES, INNER), shape(FRAMES, HEADS),
            shape(4, QROWS, WIDTH),
        ],
        scratch_shapes=[pltpu.VMEM((DIM, INNER), f32), pltpu.VMEM((8, 128), f32)],
        compiler_params=settings(62),
        cost_estimate=pl.CostEstimate(flops=4 * 10**9, bytes_accessed=12 * 2**20, transcendentals=10**6),
        name="local",
    )(frames, normed, inflow, bc_act, log, z_weight)
    arrived, inner = lax.optimization_barrier((arrived, inner))
    before = pl.pallas_call(
        scan_kernel,
        out_shape=shape(OWNERS, 8, 128),
        compiler_params=settings(16),
        name="scan",
    )(arrived)
    incoming = exchange(before).reshape(INNER, DIM)
    asked = arrived[:, 0, 1152 : 1152 + SLOTS].astype(jnp.int32)
    codes_column = asked.reshape(TOTAL, 1)
    codes_row = asked.reshape(1, TOTAL)
    found = pl.pallas_call(
        lookup_kernel,
        grid=(5,),
        in_specs=[rows_of(TOTAL // 5, 1), whole(LEVELS * CODES, WIDTH)],
        out_specs=rows_of(2 * TOTAL // 5, 128),
        out_shape=shape(2 * TOTAL, 128),
        scratch_shapes=[pltpu.VMEM((LEVELS * CODES, 2 * WIDTH), bf16)],
        compiler_params=settings(62),
        cost_estimate=pl.CostEstimate(flops=6 * 10**9, bytes_accessed=5 * 2**20, transcendentals=0),
        name="lookup",
    )(codes_column, codebook.reshape(LEVELS * CODES, WIDTH))
    fetched = exchange(found.reshape(OWNERS, 2 * SLOTS, 128)).reshape(2 * TOTAL, 128)
    shares = pl.pallas_call(
        outer_kernel,
        grid_spec=pltpu.PrefetchScalarGridSpec(
            num_scalar_prefetch=1,
            grid=(STEPS,),
            in_specs=[
                rows_of(BLOCK, INNER), rows_of(BLOCK, INNER), rows_of(BLOCK, HEADS),
                pl.BlockSpec((BLOCK, DIM), lambda i, *_: (i, 1)),
                whole(INNER, DIM), whole(1, INNER), whole(INNER, 1024),
            ],
            out_specs=[whole(QROWS, WIDTH)] * 4,
            scratch_shapes=[pltpu.VMEM((QROWS, INNER), f32)],
        ),
        out_shape=[shape(QROWS, WIDTH)] * 4,
        compiler_params=settings(62),
        cost_estimate=pl.CostEstimate(flops=2 * 10**9, bytes_accessed=8 * 2**20, transcendentals=10**5),
        name="outer",
    )(book, inner, gate, reach, bc_act, incoming, out_gain.reshape(1, -1), out_weight)
    moved = [
        lax.ppermute(shares[d], "book", [(i, (i + d) % 4) for i in range(4)]) for d in (1, 2, 3)
    ]
    terms, taken = pl.pallas_call(
        taken_kernel,
        out_shape=[shape(TOTAL, WIDTH), shape(QROWS, WIDTH)],
        compiler_params=settings(40),
        cost_estimate=pl.CostEstimate(flops=3 * 10**9, bytes_accessed=3 * 2**20, transcendentals=0),
        name="taken",
    )(fetched, slots)
    residual, grads = pl.pallas_call(
        residual_kernel,
        grid_spec=pltpu.PrefetchScalarGridSpec(
            num_scalar_prefetch=1,
            grid=(1,),
            in_specs=[whole(QROWS, WIDTH)] * 4
            + [
                pl.BlockSpec((1, QROWS, WIDTH), lambda i, book: (book[0], 0, 0)),
                whole(QROWS, WIDTH), whole(TOTAL, WIDTH), whole(LEVELS, QROWS),
            ],
            out_specs=[whole(QROWS, WIDTH), whole(2 * TOTAL, 128)],
        ),
        out_shape=[shape(QROWS, WIDTH), shape(2 * TOTAL, 128)],
        compiler_params=settings(40),
        name="residual",
    )(book, shares[0], *moved, means, taken, terms, slots)
    returned = exchange(grads.reshape(OWNERS, 2 * SLOTS, 128)).reshape(2 * TOTAL, 128)
    table = pl.pallas_call(
        table_kernel,
        grid=(6,),
        in_specs=[whole(1, TOTAL), whole(2 * TOTAL, 128)],
        out_specs=rows_of(LEVELS * CODES // 6, WIDTH),
        out_shape=shape(LEVELS * CODES, WIDTH),
        scratch_shapes=[pltpu.VMEM((TOTAL, 2 * WIDTH), bf16)],
        compiler_params=settings(40),
        name="table",
    )(codes_row, returned)
    return residual, table.reshape(LEVELS, CODES, WIDTH)


def solution(mesh):
    finer = Mesh(
        mesh.devices.reshape(8, 4, 2, mesh.shape["book"]), ("seq_0", "seq_1", "seq_2", "book")
    )
    placed = (
        P(SEQ, None), P(), P(None, "book"), P(None, "book"), P(), P(None, "book"), P("book"),
        P("book"), P("book"), P("book", None), P(None, SEQ, "book"), P(None, SEQ),
    )
    return jax.shard_map(
        body,
        mesh=finer,
        in_specs=placed,
        out_specs=(P(SEQ, "book"), P(None, SEQ, "book")),
        check_vma=False,
    )
```

```python
import jax
import jax.numpy as jnp
from jax import lax
from jax.experimental import pallas as pl
from jax.experimental.pallas import tpu as pltpu
from jax.sharding import Mesh
from jax.sharding import PartitionSpec as P

SEQ = ("seq_0", "seq_1", "seq_2")
OWNERS = 64
SLOTS = 20
TOTAL = OWNERS * SLOTS
LEVELS = 3
CODES = 1024
FRAMES = 1024
BLOCK = 256
STEPS = FRAMES // BLOCK
QROWS = 256
WIDTH = 256
HEADS = 4
DIM = 128
INNER = HEADS * DIM
PAYLOAD = 10 * 128

f32 = jnp.float32
bf16 = jnp.bfloat16
HIGHEST = lax.Precision.HIGHEST
NT = (((1,), (1,)), ((), ()))


def dot(a, b):
    return jnp.dot(a, b, preferred_element_type=f32)


def three_parts(values):
    high = values.astype(bf16)
    rest = values - high.astype(f32)
    middle = rest.astype(bf16)
    return high, middle, (rest - middle.astype(f32)).astype(bf16)


def iota(shape, dim):
    return lax.broadcasted_iota(jnp.int32, shape, dim)


def two_parts(values):
    high = values.astype(bf16)
    low = (values - high.astype(f32)).astype(bf16)
    return jnp.concatenate([high, low], axis=1)


def folded(values):
    half = values.shape[1] // 2
    return values[:, :half] + values[:, half:]


def silu(values):
    return values * jax.nn.sigmoid(values)


def per_head(columns):
    rows = columns.shape[0]
    return jnp.concatenate(
        [jnp.broadcast_to(columns[:, h : h + 1], (rows, DIM)) for h in range(HEADS)], axis=1
    )


def running_sum(causal, values):
    ones = causal.astype(bf16)
    return sum(dot(ones, part) for part in three_parts(values))


def state_step(state, decayed, cum, b_act):
    return state * per_head(jnp.exp(cum[BLOCK - 1 :, :])) + dot(b_act.T, decayed)


def place_codes(ids_ref, slots_ref):
    entries = LEVELS * QROWS
    ids = jnp.concatenate([ids_ref[k : k + 1, :] for k in range(LEVELS)], axis=1)
    level = iota((1, entries), 1) // QROWS
    owner = ids // CODES
    wanted = level * CODES + ids % CODES + 1
    member = (iota((OWNERS, entries), 0) == owner).astype(f32)
    before = (iota((QROWS, QROWS), 0) < iota((QROWS, QROWS), 1)).astype(bf16)
    seen = jnp.zeros((OWNERS, 1), f32)
    ranks = []
    for k in range(LEVELS):
        part = member[:, k * QROWS : (k + 1) * QROWS]
        ranks.append(jnp.sum(part * (dot(part.astype(bf16), before) + seen), axis=0, keepdims=True))
        seen = seen + jnp.sum(part, axis=1, keepdims=True)
    rank = jnp.concatenate(ranks, axis=1).astype(jnp.int32)
    slot = owner * SLOTS + rank
    for k in range(LEVELS):
        slots_ref[k : k + 1, :] = slot[:, k * QROWS : (k + 1) * QROWS]
    ranked = (iota((128, entries), 0) == rank).astype(bf16)
    high = (member * (wanted // 64).astype(f32)).astype(bf16)
    low = (member * (wanted % 64).astype(f32)).astype(bf16)
    return 64.0 * lax.dot_general(high, ranked, NT, preferred_element_type=f32) + lax.dot_general(
        low, ranked, NT, preferred_element_type=f32
    )


def front_kernel(
    frames_ref, gain_ref, x_w_ref, bc_w_ref, dt_w_ref, bias_ref, rate_ref, ids_ref,
    payload_ref, slots_ref, normed_ref, inflow_ref, bc_ref, log_ref,
    state_ref, total_ref,
):
    step = pl.program_id(0)

    @pl.when(step == 0)
    def _():
        state_ref[...] = jnp.zeros_like(state_ref)
        total_ref[...] = jnp.zeros_like(total_ref)
        asked = place_codes(ids_ref, slots_ref)
        for k in range(OWNERS):
            payload_ref[k, :, 1152:1280] = asked[k : k + 1, :]

    frames = frames_ref[...].astype(f32)
    square = jnp.mean(frames * frames, axis=1, keepdims=True)
    normed = (frames * lax.rsqrt(square + 1e-05) * gain_ref[...]).astype(bf16)
    normed_ref[...] = normed
    bc_act = silu(dot(normed, bc_w_ref[...]).astype(bf16).astype(f32)).astype(bf16)
    bc_ref[...] = bc_act
    raw = lax.dot_general(normed, dt_w_ref[...], NT, preferred_element_type=f32) + bias_ref[...]
    dt = jnp.maximum(raw, 0.0) + jnp.log1p(jnp.exp(-jnp.abs(raw)))
    log = -dt * rate_ref[...]
    log_ref[...] = log
    causal = iota((BLOCK, BLOCK), 0) >= iota((BLOCK, BLOCK), 1)
    cum = running_sum(causal, log)
    x_act = silu(dot(normed, x_w_ref[...]).astype(bf16).astype(f32))
    inflow = x_act * per_head(dt)
    inflow_ref[...] = inflow.astype(bf16)
    last = cum[BLOCK - 1 :, :]
    decayed = (inflow * per_head(jnp.exp(last - cum))).astype(bf16)
    state_ref[...] = state_step(state_ref[...], decayed, cum, bc_act[:, :DIM])
    total_ref[0:1, 0:HEADS] += last

    @pl.when(step == STEPS - 1)
    def _():
        for k in range(OWNERS):
            head, row = k // 16, (k % 16) * 8
            lanes = slice(head * DIM, (head + 1) * DIM)
            for r in range(8):
                payload_ref[k, :, r * 128 : (r + 1) * 128] = state_ref[row + r : row + r + 1, lanes]
            payload_ref[k, :, 1024:1152] = jnp.broadcast_to(
                total_ref[0:1, head : head + 1], (1, 128)
            )


def scan_kernel(arrived_ref, before_ref):
    carried = [jnp.zeros((1, 128), f32) for _ in range(8)]
    for k in range(OWNERS):
        decay = jnp.exp(arrived_ref[k, :, 1024:1152])
        for r in range(8):
            before_ref[k, r : r + 1, :] = carried[r]
            carried[r] = carried[r] * decay + arrived_ref[k, :, r * 128 : (r + 1) * 128]


def local_kernel(
    frames_ref, normed_ref, inflow_ref, bc_ref, log_ref, z_w_ref,
    inner_ref, gate_ref, reach_ref, means_ref,
    state_ref, total_ref,
):
    @pl.when(pl.program_id(0) == 0)
    def _():
        state_ref[...] = jnp.zeros_like(state_ref)
        total_ref[...] = jnp.zeros_like(total_ref)

    gate_ref[...] = silu(dot(normed_ref[...], z_w_ref[...]).astype(bf16).astype(f32))
    pool = jnp.where(
        iota((BLOCK // 4, BLOCK), 0) == iota((BLOCK // 4, BLOCK), 1) // 4, 0.25, 0.0
    ).astype(bf16)
    means = dot(pool, frames_ref[...])
    for g in range(4):
        means_ref[g] = means[:, g * WIDTH : (g + 1) * WIDTH]
    causal = iota((BLOCK, BLOCK), 0) >= iota((BLOCK, BLOCK), 1)
    log = log_ref[...]
    cum = running_sum(causal, log)
    cum_rows = jnp.concatenate([cum, jnp.zeros((BLOCK, 128 - HEADS), f32)], axis=1).T
    b_act, c_act = bc_ref[:, :DIM], bc_ref[:, DIM:]
    inflow = inflow_ref[...]
    scores = jnp.where(causal, lax.dot_general(c_act, b_act, NT, preferred_element_type=f32), 0.0)
    carried = dot(c_act, state_ref[...].astype(bf16)) * per_head(jnp.exp(cum))
    for h in range(HEADS):
        lanes = slice(h * DIM, (h + 1) * DIM)
        gaps = jnp.minimum(cum[:, h : h + 1] - cum_rows[h : h + 1, :], 0.0)
        mixed = (jnp.exp(gaps) * scores).astype(bf16)
        inner_ref[:, lanes] = dot(mixed, inflow[:, lanes]) + carried[:, lanes]
    reach_ref[...] = jnp.exp(cum + total_ref[0:1, 0:HEADS])
    last = cum[BLOCK - 1 :, :]
    total_ref[0:1, 0:HEADS] += last
    decayed = (inflow.astype(f32) * per_head(jnp.exp(last - cum))).astype(bf16)
    state_ref[...] = state_step(state_ref[...], decayed, cum, b_act)


def outer_kernel(
    book_ref, inner_ref, gate_ref, reach_ref, c_ref, incoming_ref, gain_ref, out_w_ref,
    out_0, out_1, out_2, out_3, pooled_ref,
):
    step = pl.program_id(0)
    pool = jnp.where(
        iota((BLOCK // 4, BLOCK), 0) == iota((BLOCK // 4, BLOCK), 1) // 4, 0.25, 0.0
    ).astype(bf16)
    c_act = c_ref[...]
    for h in range(HEADS):
        lanes = slice(h * DIM, (h + 1) * DIM)
        carried = dot(c_act, incoming_ref[lanes, :].astype(bf16))
        rows = (inner_ref[:, lanes] + carried * reach_ref[:, h : h + 1]) * gate_ref[:, lanes]
        square = jnp.mean(rows * rows, axis=1, keepdims=True)
        rows = (rows * lax.rsqrt(square + 1e-05) * gain_ref[:, lanes]).astype(bf16)
        pooled_ref[pl.ds(step * (BLOCK // 4), BLOCK // 4), lanes] = dot(pool, rows)

    @pl.when(step == STEPS - 1)
    def _():
        pooled = pooled_ref[...]
        high = pooled.astype(bf16)
        low = (pooled - high.astype(f32)).astype(bf16)
        both = jnp.concatenate([high, low], axis=0)
        for shift, out in enumerate((out_0, out_1, out_2, out_3)):
            start = pl.multiple_of(((book_ref[0] + shift) % 4) * WIDTH, WIDTH)
            product = dot(both, out_w_ref[:, pl.ds(start, WIDTH)])
            out[...] = product[:QROWS] + product[QROWS:]


def lookup_kernel(arrived_ref, table_ref, found_ref, asked_ref, columns_ref, total_ref):
    level = pl.program_id(0)

    @pl.when(level == 0)
    def _():
        for k in range(OWNERS):
            asked_ref[k : k + 1, :] = arrived_ref[k, :, 1152:1280]
        turned = asked_ref[...].T
        for k in range(OWNERS):
            columns_ref[k * SLOTS : (k + 1) * SLOTS, :] = jnp.broadcast_to(
                turned[:SLOTS, k : k + 1], (SLOTS, 128)
            )
        total_ref[...] = jnp.zeros_like(total_ref)

    first = level * CODES + 1
    place = iota((TOTAL, 128), 1) + first
    asked = columns_ref[...].astype(jnp.int32)
    chosen = jnp.concatenate(
        [(asked == place + g * 128).astype(bf16) for g in range(CODES // 128)], axis=1
    )
    total_ref[...] += dot(chosen, table_ref[0].astype(bf16))

    @pl.when(level == LEVELS - 1)
    def _():
        found_ref[pl.ds(0, TOTAL, 2), :] = total_ref[:, :128]
        found_ref[pl.ds(1, TOTAL, 2), :] = total_ref[:, 128:]


def joined_rows(ref):
    half = ref.shape[0] // 2
    return jnp.concatenate([ref[pl.ds(0, half, 2), :], ref[pl.ds(1, half, 2), :]], axis=1)


def taken_kernel(found_ref, slots_ref, terms_ref, taken_ref):
    found = joined_rows(found_ref)
    rounded = found.astype(bf16)
    slots = jnp.concatenate(
        [slots_ref[...].astype(f32), jnp.zeros((8 - LEVELS, QROWS), f32)], axis=0
    )
    same = (iota((QROWS, QROWS), 0) == iota((QROWS, QROWS), 1)).astype(f32)
    columns = lax.dot_general(same, slots, NT, preferred_element_type=f32, precision=HIGHEST)
    columns = columns.astype(jnp.int32)
    taken = jnp.zeros((QROWS, WIDTH), f32)
    terms = found
    for k in range(LEVELS):
        if k:
            spread = (iota((TOTAL, QROWS), 0) == slots_ref[k : k + 1, :]).astype(bf16)
            terms = terms + folded(dot(spread, two_parts(taken)))
        picks = (columns[:, k : k + 1] == iota((QROWS, TOTAL), 1)).astype(bf16)
        taken = taken + dot(picks, rounded)
    terms_ref[...] = terms
    taken_ref[...] = taken


def residual_kernel(
    book_ref, own_ref, from_1, from_2, from_3, means_ref, taken_ref, terms_ref, slots_ref,
    residual_ref, grads_ref,
):
    pooled = own_ref[...] + from_1[...] + from_2[...] + from_3[...] + means_ref[0]
    residual_ref[...] = pooled - taken_ref[...]
    place = iota((TOTAL, QROWS), 0)
    spread = place == slots_ref[0:1, :]
    for k in range(1, LEVELS):
        spread = spread | (place == slots_ref[k : k + 1, :])
    grads = terms_ref[...] - folded(dot(spread.astype(bf16), two_parts(pooled)))
    grads_ref[pl.ds(0, TOTAL, 2), :] = grads[:, :128]
    grads_ref[pl.ds(1, TOTAL, 2), :] = grads[:, 128:]


def table_kernel(codes_ref, grads_ref, table_ref, rounded_ref):
    step = pl.program_id(0)

    @pl.when(step == 0)
    def _():
        rounded_ref[...] = joined_rows(grads_ref).astype(bf16)

    rows = table_ref.shape[0]
    chosen = (codes_ref[...] == iota((rows, TOTAL), 0) + (step * rows + 1)).astype(bf16)
    table_ref[...] = dot(chosen, rounded_ref[...])


def shape(*dims, dtype=f32):
    return jax.ShapeDtypeStruct(dims, dtype)


def whole(*dims):
    return pl.BlockSpec(dims, lambda *_: (0,) * len(dims))


def rows_of(rows, columns):
    return pl.BlockSpec((rows, columns), lambda i, *_: (i, 0))


def settings(mib):
    return pltpu.CompilerParams(vmem_limit_bytes=mib * 2**20)


def exchange(array):
    return lax.all_to_all(array, SEQ, split_axis=0, concat_axis=0, tiled=True)


def body(
    frames, norm_gain, x_weight, z_weight, bc_weight, dt_weight, dt_bias, decay_rate,
    out_gain, out_weight, codebook, code_ids,
):
    book = lax.axis_index("book").reshape(1)
    payload, slots, normed, inflow, bc_act, log = pl.pallas_call(
        front_kernel,
        grid=(STEPS,),
        in_specs=[
            rows_of(BLOCK, 1024), whole(1, 1024), whole(1024, INNER), whole(1024, 256),
            whole(HEADS, 1024), whole(1, HEADS), whole(1, HEADS), whole(LEVELS, QROWS),
        ],
        out_specs=[
            whole(OWNERS, 1, PAYLOAD), whole(LEVELS, QROWS), rows_of(BLOCK, 1024),
            rows_of(BLOCK, INNER), rows_of(BLOCK, 256), rows_of(BLOCK, HEADS),
        ],
        out_shape=[
            shape(OWNERS, 1, PAYLOAD), shape(LEVELS, QROWS, dtype=jnp.int32),
            shape(FRAMES, 1024, dtype=bf16), shape(FRAMES, INNER, dtype=bf16),
            shape(FRAMES, 256, dtype=bf16), shape(FRAMES, HEADS),
        ],
        scratch_shapes=[pltpu.VMEM((DIM, INNER), f32), pltpu.VMEM((8, 128), f32)],
        compiler_params=settings(62),
        name="front",
    )(
        frames, norm_gain.reshape(1, -1), x_weight, bc_weight, dt_weight.T,
        dt_bias.reshape(1, -1), decay_rate.reshape(1, -1), code_ids,
    )
    arrived = exchange(payload)
    inner, gate, reach, means = pl.pallas_call(
        local_kernel,
        grid=(STEPS,),
        in_specs=[
            rows_of(BLOCK, 1024), rows_of(BLOCK, 1024), rows_of(BLOCK, INNER),
            rows_of(BLOCK, 256), rows_of(BLOCK, HEADS), whole(1024, INNER),
        ],
        out_specs=[
            rows_of(BLOCK, INNER), rows_of(BLOCK, INNER), rows_of(BLOCK, HEADS),
            pl.BlockSpec((4, BLOCK // 4, WIDTH), lambda i: (0, i, 0)),
        ],
        out_shape=[
            shape(FRAMES, INNER), shape(FRAMES, INNER), shape(FRAMES, HEADS),
            shape(4, QROWS, WIDTH),
        ],
        scratch_shapes=[pltpu.VMEM((DIM, INNER), f32), pltpu.VMEM((8, 128), f32)],
        compiler_params=settings(62),
        cost_estimate=pl.CostEstimate(flops=4 * 10**9, bytes_accessed=12 * 2**20, transcendentals=10**6),
        name="local",
    )(frames, normed, inflow, bc_act, log, z_weight)
    arrived, inner = lax.optimization_barrier((arrived, inner))
    found = pl.pallas_call(
        lookup_kernel,
        grid=(LEVELS,),
        in_specs=[
            whole(OWNERS, 1, PAYLOAD), pl.BlockSpec((1, CODES, WIDTH), lambda i: (i, 0, 0)),
        ],
        out_specs=whole(2 * TOTAL, 128),
        out_shape=shape(2 * TOTAL, 128),
        scratch_shapes=[
            pltpu.VMEM((OWNERS, 128), f32), pltpu.VMEM((TOTAL, 128), f32),
            pltpu.VMEM((TOTAL, WIDTH), f32),
        ],
        compiler_params=settings(56),
        cost_estimate=pl.CostEstimate(flops=4 * 10**9, bytes_accessed=5 * 2**20, transcendentals=0),
        name="lookup",
    )(arrived, codebook)
    fetched = exchange(found.reshape(OWNERS, 2 * SLOTS, 128)).reshape(2 * TOTAL, 128)
    before = pl.pallas_call(
        scan_kernel,
        out_shape=shape(OWNERS, 8, 128),
        compiler_params=settings(16),
        name="scan",
    )(arrived)
    incoming = exchange(before).reshape(INNER, DIM)
    shares = pl.pallas_call(
        outer_kernel,
        grid_spec=pltpu.PrefetchScalarGridSpec(
            num_scalar_prefetch=1,
            grid=(STEPS,),
            in_specs=[
                rows_of(BLOCK, INNER), rows_of(BLOCK, INNER), rows_of(BLOCK, HEADS),
                pl.BlockSpec((BLOCK, DIM), lambda i, *_: (i, 1)),
                whole(INNER, DIM), whole(1, INNER), whole(INNER, 1024),
            ],
            out_specs=[whole(QROWS, WIDTH)] * 4,
            scratch_shapes=[pltpu.VMEM((QROWS, INNER), f32)],
        ),
        out_shape=[shape(QROWS, WIDTH)] * 4,
        compiler_params=settings(62),
        cost_estimate=pl.CostEstimate(flops=2 * 10**9, bytes_accessed=8 * 2**20, transcendentals=10**5),
        name="outer",
    )(book, inner, gate, reach, bc_act, incoming, out_gain.reshape(1, -1), out_weight)
    moved = [
        lax.ppermute(shares[d], "book", [(i, (i + d) % 4) for i in range(4)]) for d in (1, 2, 3)
    ]
    terms, taken = pl.pallas_call(
        taken_kernel,
        out_shape=[shape(TOTAL, WIDTH), shape(QROWS, WIDTH)],
        compiler_params=settings(40),
        cost_estimate=pl.CostEstimate(flops=3 * 10**9, bytes_accessed=3 * 2**20, transcendentals=0),
        name="taken",
    )(fetched, slots)
    residual, grads = pl.pallas_call(
        residual_kernel,
        grid_spec=pltpu.PrefetchScalarGridSpec(
            num_scalar_prefetch=1,
            grid=(1,),
            in_specs=[whole(QROWS, WIDTH)] * 4
            + [
                pl.BlockSpec((1, QROWS, WIDTH), lambda i, book: (book[0], 0, 0)),
                whole(QROWS, WIDTH), whole(TOTAL, WIDTH), whole(LEVELS, QROWS),
            ],
            out_specs=[whole(QROWS, WIDTH), whole(2 * TOTAL, 128)],
        ),
        out_shape=[shape(QROWS, WIDTH), shape(2 * TOTAL, 128)],
        compiler_params=settings(40),
        name="residual",
    )(book, shares[0], *moved, means, taken, terms, slots)
    returned = exchange(grads.reshape(OWNERS, 2 * SLOTS, 128)).reshape(2 * TOTAL, 128)
    arrived, grads = lax.optimization_barrier((arrived, grads))
    codes = arrived[:, 0, 1152 : 1152 + SLOTS].astype(jnp.int32).reshape(1, TOTAL)
    table = pl.pallas_call(
        table_kernel,
        grid=(6,),
        in_specs=[whole(1, TOTAL), whole(2 * TOTAL, 128)],
        out_specs=rows_of(LEVELS * CODES // 6, WIDTH),
        out_shape=shape(LEVELS * CODES, WIDTH),
        scratch_shapes=[pltpu.VMEM((TOTAL, WIDTH), bf16)],
        compiler_params=settings(40),
        name="table",
    )(codes, returned)
    return residual, table.reshape(LEVELS, CODES, WIDTH)


def solution(mesh):
    finer = Mesh(
        mesh.devices.reshape(8, 4, 2, mesh.shape["book"]), ("seq_0", "seq_1", "seq_2", "book")
    )
    placed = (
        P(SEQ, None), P(), P(None, "book"), P(None, "book"), P(), P(None, "book"), P("book"),
        P("book"), P("book"), P("book", None), P(None, SEQ, "book"), P(None, SEQ),
    )
    return jax.shard_map(
        body,
        mesh=finer,
        in_specs=placed,
        out_specs=(P(SEQ, "book"), P(None, SEQ, "book")),
        check_vma=False,
    )
```

```python
import functools

import jax
import jax.numpy as jnp
from jax import lax
from jax.experimental import pallas as pl
from jax.experimental.pallas import tpu as pltpu
from jax.sharding import Mesh
from jax.sharding import PartitionSpec as P

SEQ = ("seq_0", "seq_1", "seq_2")
OWNERS = 64
SLOTS = 20
FEW = 16
LATE = SLOTS - FEW
LEVELS = 3
LOW = 4
CODES = 1024
FRAMES = 1024
BLOCK = 256
STEPS = FRAMES // BLOCK
QROWS = 256
WIDTH = 256
HEADS = 4
DIM = 128
INNER = HEADS * DIM
PAYLOAD = 10 * 128

f32 = jnp.float32
bf16 = jnp.bfloat16
HIGHEST = lax.Precision.HIGHEST
NT = (((1,), (1,)), ((), ()))


def dot(a, b):
    return jnp.dot(a, b, preferred_element_type=f32)


def three_parts(values):
    high = values.astype(bf16)
    rest = values - high.astype(f32)
    middle = rest.astype(bf16)
    return high, middle, (rest - middle.astype(f32)).astype(bf16)


def iota(shape, dim):
    return lax.broadcasted_iota(jnp.int32, shape, dim)


def two_parts(values):
    high = values.astype(bf16)
    low = (values - high.astype(f32)).astype(bf16)
    return jnp.concatenate([high, low], axis=1)


def folded(values):
    half = values.shape[1] // 2
    return values[:, :half] + values[:, half:]


def silu(values):
    return values * jax.nn.sigmoid(values)


def per_head(columns):
    rows = columns.shape[0]
    return jnp.concatenate(
        [jnp.broadcast_to(columns[:, h : h + 1], (rows, DIM)) for h in range(HEADS)], axis=1
    )


def running_sum(causal, values):
    ones = causal.astype(bf16)
    return sum(dot(ones, part) for part in three_parts(values))


def state_step(state, decayed, cum, b_act):
    return state * per_head(jnp.exp(cum[BLOCK - 1 :, :])) + dot(b_act.T, decayed)


def place_codes(ids_ref, slots_ref, few_ref, hot_ref):
    entries = LEVELS * QROWS
    ids = jnp.concatenate([ids_ref[k : k + 1, :] for k in range(LEVELS)], axis=1)
    level = iota((1, entries), 1) // QROWS
    owner = ids // CODES
    wanted = level * CODES + ids % CODES + 1
    member = (iota((OWNERS, entries), 0) == owner).astype(f32)
    before = (iota((QROWS, QROWS), 0) < iota((QROWS, QROWS), 1)).astype(bf16)
    seen = jnp.zeros((OWNERS, 1), f32)
    hot = jnp.zeros((OWNERS, 1), f32)
    ranks = []
    for k in range(LEVELS):
        part = member[:, k * QROWS : (k + 1) * QROWS]
        ranks.append(jnp.sum(part * (dot(part.astype(bf16), before) + seen), axis=0, keepdims=True))
        count = jnp.sum(part, axis=1, keepdims=True)
        seen = seen + count
        hot = jnp.maximum(hot, jnp.where(count > LOW, 1.0, 0.0))
    rank = jnp.concatenate(ranks, axis=1).astype(jnp.int32)
    slot = owner * SLOTS + rank
    neighbour = owner + 1 - 2 * (owner % 2)
    few = jnp.where(rank < FEW, owner * FEW + rank, neighbour * FEW + rank - LATE)
    for k in range(LEVELS):
        slots_ref[k : k + 1, :] = slot[:, k * QROWS : (k + 1) * QROWS]
        few_ref[k : k + 1, :] = few[:, k * QROWS : (k + 1) * QROWS]
    chip = (iota((OWNERS // 2, OWNERS), 0) == iota((OWNERS // 2, OWNERS), 1) // 2).astype(bf16)
    on_chip = dot(chip, jnp.broadcast_to(hot, (OWNERS, 128)).astype(bf16))
    hot_ref[...] = jnp.max(on_chip, axis=0, keepdims=True)
    ranked = (iota((128, entries), 0) == rank).astype(bf16)
    high = (member * (wanted // 64).astype(f32)).astype(bf16)
    low = (member * (wanted % 64).astype(f32)).astype(bf16)
    return 64.0 * lax.dot_general(high, ranked, NT, preferred_element_type=f32) + lax.dot_general(
        low, ranked, NT, preferred_element_type=f32
    )


def front_kernel(
    frames_ref, gain_ref, x_w_ref, bc_w_ref, dt_w_ref, bias_ref, rate_ref, ids_ref,
    payload_ref, slots_ref, few_ref, hot_ref, normed_ref, inflow_ref, bc_ref, log_ref,
    state_ref, total_ref,
):
    step = pl.program_id(0)

    @pl.when(step == 0)
    def _():
        state_ref[...] = jnp.zeros_like(state_ref)
        total_ref[...] = jnp.zeros_like(total_ref)
        asked = place_codes(ids_ref, slots_ref, few_ref, hot_ref)
        for k in range(OWNERS):
            payload_ref[k, :, 1152:1280] = asked[k : k + 1, :]

    frames = frames_ref[...].astype(f32)
    square = jnp.mean(frames * frames, axis=1, keepdims=True)
    normed = (frames * lax.rsqrt(square + 1e-05) * gain_ref[...]).astype(bf16)
    normed_ref[...] = normed
    bc_act = silu(dot(normed, bc_w_ref[...]).astype(bf16).astype(f32)).astype(bf16)
    bc_ref[...] = bc_act
    raw = lax.dot_general(normed, dt_w_ref[...], NT, preferred_element_type=f32) + bias_ref[...]
    dt = jnp.maximum(raw, 0.0) + jnp.log1p(jnp.exp(-jnp.abs(raw)))
    log = -dt * rate_ref[...]
    log_ref[...] = log
    causal = iota((BLOCK, BLOCK), 0) >= iota((BLOCK, BLOCK), 1)
    cum = running_sum(causal, log)
    x_act = silu(dot(normed, x_w_ref[...]).astype(bf16).astype(f32))
    inflow = x_act * per_head(dt)
    inflow_ref[...] = inflow.astype(bf16)
    last = cum[BLOCK - 1 :, :]
    decayed = (inflow * per_head(jnp.exp(last - cum))).astype(bf16)
    state_ref[...] = state_step(state_ref[...], decayed, cum, bc_act[:, :DIM])
    total_ref[0:1, 0:HEADS] += last

    @pl.when(step == STEPS - 1)
    def _():
        for k in range(OWNERS):
            head, row = k // 16, (k % 16) * 8
            lanes = slice(head * DIM, (head + 1) * DIM)
            for r in range(8):
                payload_ref[k, :, r * 128 : (r + 1) * 128] = state_ref[row + r : row + r + 1, lanes]
            payload_ref[k, :, 1024:1152] = jnp.broadcast_to(
                total_ref[0:1, head : head + 1], (1, 128)
            )


def scan_kernel(arrived_ref, before_ref):
    carried = [jnp.zeros((1, 128), f32) for _ in range(8)]
    for k in range(OWNERS):
        decay = jnp.exp(arrived_ref[k, :, 1024:1152])
        for r in range(8):
            before_ref[k, r : r + 1, :] = carried[r]
            carried[r] = carried[r] * decay + arrived_ref[k, :, r * 128 : (r + 1) * 128]


def local_kernel(
    frames_ref, normed_ref, inflow_ref, bc_ref, log_ref, z_w_ref,
    inner_ref, gate_ref, reach_ref, means_ref,
    state_ref, total_ref,
):
    @pl.when(pl.program_id(0) == 0)
    def _():
        state_ref[...] = jnp.zeros_like(state_ref)
        total_ref[...] = jnp.zeros_like(total_ref)

    gate_ref[...] = silu(dot(normed_ref[...], z_w_ref[...]).astype(bf16).astype(f32))
    pool = jnp.where(
        iota((BLOCK // 4, BLOCK), 0) == iota((BLOCK // 4, BLOCK), 1) // 4, 0.25, 0.0
    ).astype(bf16)
    means = dot(pool, frames_ref[...])
    for g in range(4):
        means_ref[g] = means[:, g * WIDTH : (g + 1) * WIDTH]
    causal = iota((BLOCK, BLOCK), 0) >= iota((BLOCK, BLOCK), 1)
    log = log_ref[...]
    cum = running_sum(causal, log)
    cum_rows = jnp.concatenate([cum, jnp.zeros((BLOCK, 128 - HEADS), f32)], axis=1).T
    b_act, c_act = bc_ref[:, :DIM], bc_ref[:, DIM:]
    inflow = inflow_ref[...]
    scores = jnp.where(causal, lax.dot_general(c_act, b_act, NT, preferred_element_type=f32), 0.0)
    carried = dot(c_act, state_ref[...].astype(bf16)) * per_head(jnp.exp(cum))
    for h in range(HEADS):
        lanes = slice(h * DIM, (h + 1) * DIM)
        gaps = jnp.minimum(cum[:, h : h + 1] - cum_rows[h : h + 1, :], 0.0)
        mixed = (jnp.exp(gaps) * scores).astype(bf16)
        inner_ref[:, lanes] = dot(mixed, inflow[:, lanes]) + carried[:, lanes]
    reach_ref[...] = jnp.exp(cum + total_ref[0:1, 0:HEADS])
    last = cum[BLOCK - 1 :, :]
    total_ref[0:1, 0:HEADS] += last
    decayed = (inflow.astype(f32) * per_head(jnp.exp(last - cum))).astype(bf16)
    state_ref[...] = state_step(state_ref[...], decayed, cum, b_act)


def outer_kernel(
    book_ref, inner_ref, gate_ref, reach_ref, c_ref, incoming_ref, gain_ref, out_w_ref,
    out_0, out_1, out_2, out_3, pooled_ref,
):
    step = pl.program_id(0)
    pool = jnp.where(
        iota((BLOCK // 4, BLOCK), 0) == iota((BLOCK // 4, BLOCK), 1) // 4, 0.25, 0.0
    ).astype(bf16)
    c_act = c_ref[...]
    for h in range(HEADS):
        lanes = slice(h * DIM, (h + 1) * DIM)
        carried = dot(c_act, incoming_ref[lanes, :].astype(bf16))
        rows = (inner_ref[:, lanes] + carried * reach_ref[:, h : h + 1]) * gate_ref[:, lanes]
        square = jnp.mean(rows * rows, axis=1, keepdims=True)
        rows = (rows * lax.rsqrt(square + 1e-05) * gain_ref[:, lanes]).astype(bf16)
        pooled_ref[pl.ds(step * (BLOCK // 4), BLOCK // 4), lanes] = dot(pool, rows)

    @pl.when(step == STEPS - 1)
    def _():
        pooled = pooled_ref[...]
        high = pooled.astype(bf16)
        low = (pooled - high.astype(f32)).astype(bf16)
        both = jnp.concatenate([high, low], axis=0)
        for shift, out in enumerate((out_0, out_1, out_2, out_3)):
            start = pl.multiple_of(((book_ref[0] + shift) % 4) * WIDTH, WIDTH)
            product = dot(both, out_w_ref[:, pl.ds(start, WIDTH)])
            out[...] = product[:QROWS] + product[QROWS:]


def split_rows(ref, values):
    rows = values.shape[0]
    ref[pl.ds(0, rows, 2), :] = values[:, :128]
    ref[pl.ds(1, rows, 2), :] = values[:, 128:]


def lookup_kernel(cuts, arrived_ref, table_ref, *refs):
    founds, (asked_ref, columns_ref, total_ref) = refs[: len(cuts)], refs[len(cuts) :]
    level = pl.program_id(0)

    @pl.when(level == 0)
    def _():
        for k in range(OWNERS):
            asked_ref[k : k + 1, :] = arrived_ref[k, :, 1152:1280]
        turned = asked_ref[...].T
        start = 0
        for low, high in cuts:
            for k in range(OWNERS):
                columns_ref[start : start + high - low, :] = jnp.broadcast_to(
                    turned[low:high, k : k + 1], (high - low, 128)
                )
                start += high - low
        total_ref[...] = jnp.zeros_like(total_ref)

    place = iota((OWNERS * SLOTS, 128), 1) + (level * CODES + 1)
    asked = columns_ref[...].astype(jnp.int32)
    chosen = jnp.concatenate(
        [(asked == place + g * 128).astype(bf16) for g in range(CODES // 128)], axis=1
    )
    total_ref[...] += dot(chosen, table_ref[0].astype(bf16))

    @pl.when(level == LEVELS - 1)
    def _():
        for (low, high), found_ref in zip(cuts, founds):
            split_rows(found_ref, total_ref[OWNERS * low : OWNERS * high, :])


def joined_rows(ref):
    half = ref.shape[0] // 2
    return jnp.concatenate([ref[pl.ds(0, half, 2), :], ref[pl.ds(1, half, 2), :]], axis=1)


def taken_kernel(found_ref, slots_ref, terms_ref, taken_ref):
    found = joined_rows(found_ref)
    total = found.shape[0]
    rounded = found.astype(bf16)
    slots = jnp.concatenate(
        [slots_ref[...].astype(f32), jnp.zeros((8 - LEVELS, QROWS), f32)], axis=0
    )
    same = (iota((QROWS, QROWS), 0) == iota((QROWS, QROWS), 1)).astype(f32)
    columns = lax.dot_general(same, slots, NT, preferred_element_type=f32, precision=HIGHEST)
    columns = columns.astype(jnp.int32)
    taken = jnp.zeros((QROWS, WIDTH), f32)
    terms = found
    for k in range(LEVELS):
        if k:
            spread = (iota((total, QROWS), 0) == slots_ref[k : k + 1, :]).astype(bf16)
            terms = terms + folded(dot(spread, two_parts(taken)))
        picks = (columns[:, k : k + 1] == iota((QROWS, total), 1)).astype(bf16)
        taken = taken + dot(picks, rounded)
    terms_ref[...] = terms
    taken_ref[...] = taken


def residual_kernel(
    book_ref, own_ref, from_1, from_2, from_3, means_ref, taken_ref, terms_ref, slots_ref,
    residual_ref, grads_ref,
):
    pooled = own_ref[...] + from_1[...] + from_2[...] + from_3[...] + means_ref[0]
    residual_ref[...] = pooled - taken_ref[...]
    place = iota((terms_ref.shape[0], QROWS), 0)
    spread = place == slots_ref[0:1, :]
    for k in range(1, LEVELS):
        spread = spread | (place == slots_ref[k : k + 1, :])
    grads = terms_ref[...] - folded(dot(spread.astype(bf16), two_parts(pooled)))
    split_rows(grads_ref, grads)


def table_kernel(codes_ref, *refs):
    grads_refs, (table_ref, rounded_ref) = refs[:-2], refs[-2:]
    step = pl.program_id(0)

    @pl.when(step == 0)
    def _():
        start = 0
        for grads_ref in grads_refs:
            rows = grads_ref.shape[0] // 2
            rounded_ref[start : start + rows, :] = joined_rows(grads_ref).astype(bf16)
            start += rows

    rows = table_ref.shape[0]
    place = iota((rows, codes_ref.shape[1]), 0) + (step * rows + 1)
    chosen = (codes_ref[...] == place).astype(bf16)
    table_ref[...] = dot(chosen, rounded_ref[...])


def shape(*dims, dtype=f32):
    return jax.ShapeDtypeStruct(dims, dtype)


def whole(*dims):
    return pl.BlockSpec(dims, lambda *_: (0,) * len(dims))


def rows_of(rows, columns):
    return pl.BlockSpec((rows, columns), lambda i, *_: (i, 0))


def settings(mib):
    return pltpu.CompilerParams(vmem_limit_bytes=mib * 2**20)


def exchange(array):
    return lax.all_to_all(array, SEQ, split_axis=0, concat_axis=0, tiled=True)


def looked_up(arrived, codebook, cuts):
    return pl.pallas_call(
        functools.partial(lookup_kernel, cuts),
        grid=(LEVELS,),
        in_specs=[
            whole(OWNERS, 1, PAYLOAD), pl.BlockSpec((1, CODES, WIDTH), lambda i: (i, 0, 0)),
        ],
        out_specs=[whole(2 * OWNERS * (high - low), 128) for low, high in cuts],
        out_shape=[shape(2 * OWNERS * (high - low), 128) for low, high in cuts],
        scratch_shapes=[
            pltpu.VMEM((OWNERS, 128), f32), pltpu.VMEM((OWNERS * SLOTS, 128), f32),
            pltpu.VMEM((OWNERS * SLOTS, WIDTH), f32),
        ],
        compiler_params=settings(62),
        cost_estimate=pl.CostEstimate(flops=4 * 10**9, bytes_accessed=5 * 2**20, transcendentals=0),
        name="lookup",
    )(arrived, codebook)


def scanned(arrived):
    before = pl.pallas_call(
        scan_kernel,
        out_shape=shape(OWNERS, 8, 128),
        compiler_params=settings(16),
        name="scan",
    )(arrived)
    arrived, before = lax.optimization_barrier((arrived, before))
    return exchange(before).reshape(INNER, DIM), arrived


def shared_out(book, incoming, inner, gate, reach, bc_act, out_gain, out_weight):
    shares = pl.pallas_call(
        outer_kernel,
        grid_spec=pltpu.PrefetchScalarGridSpec(
            num_scalar_prefetch=1,
            grid=(STEPS,),
            in_specs=[
                rows_of(BLOCK, INNER), rows_of(BLOCK, INNER), rows_of(BLOCK, HEADS),
                pl.BlockSpec((BLOCK, DIM), lambda i, *_: (i, 1)),
                whole(INNER, DIM), whole(1, INNER), whole(INNER, 1024),
            ],
            out_specs=[whole(QROWS, WIDTH)] * 4,
            scratch_shapes=[pltpu.VMEM((QROWS, INNER), f32)],
        ),
        out_shape=[shape(QROWS, WIDTH)] * 4,
        compiler_params=settings(62),
        cost_estimate=pl.CostEstimate(flops=2 * 10**9, bytes_accessed=8 * 2**20, transcendentals=10**5),
        name="outer",
    )(book, inner, gate, reach, bc_act, incoming, out_gain.reshape(1, -1), out_weight)
    moved = [
        lax.ppermute(shares[d], "book", [(i, (i + d) % 4) for i in range(4)]) for d in (1, 2, 3)
    ]
    return [shares[0], *moved]


def gradient_terms(book, found, slots, shares, means):
    fetched = exchange(found)
    total = OWNERS * found.shape[1] // 2
    terms, taken = pl.pallas_call(
        taken_kernel,
        out_shape=[shape(total, WIDTH), shape(QROWS, WIDTH)],
        compiler_params=settings(40),
        cost_estimate=pl.CostEstimate(flops=3 * 10**9, bytes_accessed=3 * 2**20, transcendentals=0),
        name="taken",
    )(fetched.reshape(2 * total, 128), slots)
    residual, grads = pl.pallas_call(
        residual_kernel,
        grid_spec=pltpu.PrefetchScalarGridSpec(
            num_scalar_prefetch=1,
            grid=(1,),
            in_specs=[whole(QROWS, WIDTH)] * 4
            + [
                pl.BlockSpec((1, QROWS, WIDTH), lambda i, book: (book[0], 0, 0)),
                whole(QROWS, WIDTH), whole(total, WIDTH), whole(LEVELS, QROWS),
            ],
            out_specs=[whole(QROWS, WIDTH), whole(2 * total, 128)],
        ),
        out_shape=[shape(QROWS, WIDTH), shape(2 * total, 128)],
        compiler_params=settings(40),
        name="residual",
    )(book, *shares, means, taken, terms, slots)
    return residual, grads.reshape(found.shape)


def gathered_table(codes, *grads):
    return pl.pallas_call(
        table_kernel,
        grid=(6,),
        in_specs=[whole(*codes.shape)] + [whole(*part.shape) for part in grads],
        out_specs=rows_of(LEVELS * CODES // 6, WIDTH),
        out_shape=shape(LEVELS * CODES, WIDTH),
        scratch_shapes=[pltpu.VMEM((codes.shape[1], WIDTH), bf16)],
        compiler_params=settings(40),
        name="table",
    )(codes, *grads)


def asked_codes(arrived, low, high):
    return arrived[:, 0, 1152 + low : 1152 + high].astype(jnp.int32).reshape(1, -1)


def other_core(array):
    return lax.ppermute(array, "seq_2", [(0, 1), (1, 0)])


def with_all_slots(
    book, arrived, few, slots, inner, gate, reach, means, bc_act, out_gain, out_weight, codebook
):
    incoming, arrived = scanned(arrived)
    [found] = looked_up(arrived, codebook, [(0, SLOTS)])
    shares = shared_out(book, incoming, inner, gate, reach, bc_act, out_gain, out_weight)
    residual, grads = gradient_terms(
        book, found.reshape(OWNERS, 2 * SLOTS, 128), slots, shares, means
    )
    arrived, grads = lax.optimization_barrier((arrived, grads))
    returned = exchange(grads).reshape(-1, 128)
    return residual, gathered_table(asked_codes(arrived, 0, SLOTS), returned)


def with_few_slots(
    book, arrived, few, slots, inner, gate, reach, means, bc_act, out_gain, out_weight, codebook
):
    incoming, arrived = scanned(arrived)
    found, late = looked_up(arrived, codebook, [(0, FEW), (FEW, SLOTS)])
    late, incoming = lax.optimization_barrier((late, incoming))
    late = other_core(late).reshape(OWNERS, 2 * LATE, 128)
    found = found.reshape(OWNERS, 2 * FEW, 128)
    found = found + jnp.pad(late, ((0, 0), (2 * (FEW - LATE), 0), (0, 0)))
    shares = shared_out(book, incoming, inner, gate, reach, bc_act, out_gain, out_weight)
    residual, grads = gradient_terms(book, found, few, shares, means)
    arrived, grads = lax.optimization_barrier((arrived, grads))
    codes = jnp.concatenate(
        [asked_codes(arrived, 0, FEW), asked_codes(arrived, FEW, SLOTS)], axis=1
    )
    returned = exchange(grads)
    late = other_core(returned[:, 2 * (FEW - LATE) :].reshape(-1, 128))
    return residual, gathered_table(codes, returned.reshape(-1, 128), late)


def body(
    frames, norm_gain, x_weight, z_weight, bc_weight, dt_weight, dt_bias, decay_rate,
    out_gain, out_weight, codebook, code_ids,
):
    book = lax.axis_index("book").reshape(1)
    payload, slots, few, hot, normed, inflow, bc_act, log = pl.pallas_call(
        front_kernel,
        grid=(STEPS,),
        in_specs=[
            rows_of(BLOCK, 1024), whole(1, 1024), whole(1024, INNER), whole(1024, 256),
            whole(HEADS, 1024), whole(1, HEADS), whole(1, HEADS), whole(LEVELS, QROWS),
        ],
        out_specs=[
            whole(OWNERS, 1, PAYLOAD), whole(LEVELS, QROWS), whole(LEVELS, QROWS),
            whole(1, 128), rows_of(BLOCK, 1024),
            rows_of(BLOCK, INNER), rows_of(BLOCK, 256), rows_of(BLOCK, HEADS),
        ],
        out_shape=[
            shape(OWNERS, 1, PAYLOAD), shape(LEVELS, QROWS, dtype=jnp.int32),
            shape(LEVELS, QROWS, dtype=jnp.int32), shape(1, 128),
            shape(FRAMES, 1024, dtype=bf16), shape(FRAMES, INNER, dtype=bf16),
            shape(FRAMES, 256, dtype=bf16), shape(FRAMES, HEADS),
        ],
        scratch_shapes=[pltpu.VMEM((DIM, INNER), f32), pltpu.VMEM((8, 128), f32)],
        compiler_params=settings(62),
        name="front",
    )(
        frames, norm_gain.reshape(1, -1), x_weight, bc_weight, dt_weight.T,
        dt_bias.reshape(1, -1), decay_rate.reshape(1, -1), code_ids,
    )
    arrived = exchange(payload)
    inner, gate, reach, means = pl.pallas_call(
        local_kernel,
        grid=(STEPS,),
        in_specs=[
            rows_of(BLOCK, 1024), rows_of(BLOCK, 1024), rows_of(BLOCK, INNER),
            rows_of(BLOCK, 256), rows_of(BLOCK, HEADS), whole(1024, INNER),
        ],
        out_specs=[
            rows_of(BLOCK, INNER), rows_of(BLOCK, INNER), rows_of(BLOCK, HEADS),
            pl.BlockSpec((4, BLOCK // 4, WIDTH), lambda i: (0, i, 0)),
        ],
        out_shape=[
            shape(FRAMES, INNER), shape(FRAMES, INNER), shape(FRAMES, HEADS),
            shape(4, QROWS, WIDTH),
        ],
        scratch_shapes=[pltpu.VMEM((DIM, INNER), f32), pltpu.VMEM((8, 128), f32)],
        compiler_params=settings(62),
        cost_estimate=pl.CostEstimate(flops=4 * 10**9, bytes_accessed=12 * 2**20, transcendentals=10**6),
        name="local",
    )(frames, normed, inflow, bc_act, log, z_weight)
    arrived, inner = lax.optimization_barrier((arrived, inner))
    residual, table = lax.cond(
        hot[0, 0] < 1.5, with_few_slots, with_all_slots,
        book, arrived, few, slots, inner, gate, reach, means, bc_act, out_gain, out_weight, codebook,
    )
    return residual, table.reshape(LEVELS, CODES, WIDTH)


def solution(mesh):
    finer = Mesh(
        mesh.devices.reshape(8, 4, 2, mesh.shape["book"]), ("seq_0", "seq_1", "seq_2", "book")
    )
    placed = (
        P(SEQ, None), P(), P(None, "book"), P(None, "book"), P(), P(None, "book"), P("book"),
        P("book"), P("book"), P("book", None), P(None, SEQ, "book"), P(None, SEQ),
    )
    return jax.shard_map(
        body,
        mesh=finer,
        in_specs=placed,
        out_specs=(P(SEQ, "book"), P(None, SEQ, "book")),
        check_vma=False,
    )
```

```python
import functools

import jax
import jax.numpy as jnp
from jax import lax
from jax.experimental import pallas as pl
from jax.experimental.pallas import tpu as pltpu
from jax.sharding import Mesh
from jax.sharding import PartitionSpec as P

SEQ = ("seq_0", "seq_1", "seq_2")
OWNERS = 64
SLOTS = 20
FEW = 16
LATE = SLOTS - FEW
LEVELS = 3
LOW = 4
CODES = 1024
FRAMES = 1024
BLOCK = 256
STEPS = FRAMES // BLOCK
QROWS = 256
WIDTH = 256
HEADS = 4
DIM = 128
INNER = HEADS * DIM
PAYLOAD = 9 * 128
ASKED = 8 * 128

f32 = jnp.float32
bf16 = jnp.bfloat16
HIGHEST = lax.Precision.HIGHEST
NT = (((1,), (1,)), ((), ()))


def dot(a, b):
    return jnp.dot(a, b, preferred_element_type=f32)


def three_parts(values):
    high = values.astype(bf16)
    rest = values - high.astype(f32)
    middle = rest.astype(bf16)
    return high, middle, (rest - middle.astype(f32)).astype(bf16)


def iota(shape, dim):
    return lax.broadcasted_iota(jnp.int32, shape, dim)


def two_parts(values):
    high = values.astype(bf16)
    low = (values - high.astype(f32)).astype(bf16)
    return jnp.concatenate([high, low], axis=1)


def folded(values):
    half = values.shape[1] // 2
    return values[:, :half] + values[:, half:]


def silu(values):
    return values * jax.nn.sigmoid(values)


def filled(columns):
    return jnp.concatenate([columns, jnp.zeros((columns.shape[0], 128 - HEADS), f32)], axis=1)


def per_head(columns):
    rows = columns.shape[0]
    return jnp.concatenate(
        [jnp.broadcast_to(columns[:, h : h + 1], (rows, DIM)) for h in range(HEADS)], axis=1
    )


def running_sum(causal, values):
    ones = causal.astype(bf16)
    return sum(dot(ones, part) for part in three_parts(values))


def state_step(state, decayed, cum, b_act):
    return state * per_head(jnp.exp(cum[BLOCK - 1 :, :])) + dot(b_act.T, decayed)


def place_codes(ids_ref, slots_ref, few_ref, hot_ref):
    entries = LEVELS * QROWS
    ids = jnp.concatenate([ids_ref[k : k + 1, :] for k in range(LEVELS)], axis=1)
    level = iota((1, entries), 1) // QROWS
    owner = ids // CODES
    wanted = level * CODES + ids % CODES + 1
    member = (iota((OWNERS, entries), 0) == owner).astype(f32)
    before = (iota((QROWS, QROWS), 0) < iota((QROWS, QROWS), 1)).astype(bf16)
    seen = jnp.zeros((OWNERS, 1), f32)
    hot = jnp.zeros((OWNERS, 1), f32)
    ranks = []
    for k in range(LEVELS):
        part = member[:, k * QROWS : (k + 1) * QROWS]
        ranks.append(jnp.sum(part * (dot(part.astype(bf16), before) + seen), axis=0, keepdims=True))
        count = jnp.sum(part, axis=1, keepdims=True)
        seen = seen + count
        hot = jnp.maximum(hot, jnp.where(count > LOW, 1.0, 0.0))
    rank = jnp.concatenate(ranks, axis=1).astype(jnp.int32)
    slot = owner * SLOTS + rank
    neighbour = owner + 1 - 2 * (owner % 2)
    few = jnp.where(rank < FEW, owner * FEW + rank, neighbour * FEW + rank - LATE)
    for k in range(LEVELS):
        slots_ref[k : k + 1, :] = slot[:, k * QROWS : (k + 1) * QROWS]
        few_ref[k : k + 1, :] = few[:, k * QROWS : (k + 1) * QROWS]
    chip = (iota((OWNERS // 2, OWNERS), 0) == iota((OWNERS // 2, OWNERS), 1) // 2).astype(bf16)
    on_chip = dot(chip, jnp.broadcast_to(hot, (OWNERS, 128)).astype(bf16))
    hot_ref[...] = jnp.max(on_chip, axis=0, keepdims=True)
    ranked = (iota((128, entries), 0) == rank).astype(bf16)
    high = (member * (wanted // 64).astype(f32)).astype(bf16)
    low = (member * (wanted % 64).astype(f32)).astype(bf16)
    return 64.0 * lax.dot_general(high, ranked, NT, preferred_element_type=f32) + lax.dot_general(
        low, ranked, NT, preferred_element_type=f32
    )


def front_kernel(
    frames_ref, gain_ref, x_w_ref, bc_w_ref, dt_w_ref, bias_ref, rate_ref, ids_ref,
    payload_ref, slots_ref, few_ref, hot_ref, normed_ref, inflow_ref, bc_ref, log_ref,
    state_ref, total_ref,
):
    step = pl.program_id(0)

    @pl.when(step == 0)
    def _():
        state_ref[...] = jnp.zeros_like(state_ref)
        total_ref[...] = jnp.zeros_like(total_ref)
        asked = place_codes(ids_ref, slots_ref, few_ref, hot_ref)
        for k in range(OWNERS):
            payload_ref[k, :, ASKED:] = asked[k : k + 1, :]

    frames = frames_ref[...].astype(f32)
    square = jnp.mean(frames * frames, axis=1, keepdims=True)
    normed = (frames * lax.rsqrt(square + 1e-05) * gain_ref[...]).astype(bf16)
    normed_ref[...] = normed
    bc_act = silu(dot(normed, bc_w_ref[...]).astype(bf16).astype(f32)).astype(bf16)
    bc_ref[...] = bc_act
    raw = lax.dot_general(normed, dt_w_ref[...], NT, preferred_element_type=f32) + bias_ref[...]
    dt = jnp.maximum(raw, 0.0) + jnp.log1p(jnp.exp(-jnp.abs(raw)))
    log = -dt * rate_ref[...]
    log_ref[...] = filled(log)
    causal = iota((BLOCK, BLOCK), 0) >= iota((BLOCK, BLOCK), 1)
    cum = running_sum(causal, log)
    x_act = silu(dot(normed, x_w_ref[...]).astype(bf16).astype(f32))
    inflow = x_act * per_head(dt)
    inflow_ref[...] = inflow.astype(bf16)
    last = cum[BLOCK - 1 :, :]
    decayed = (inflow * per_head(jnp.exp(last - cum))).astype(bf16)
    state_ref[...] = state_step(state_ref[...], decayed, cum, bc_act[:, :DIM])
    total_ref[0:1, 0:HEADS] += last

    @pl.when(step == STEPS - 1)
    def _():
        for k in range(OWNERS):
            head, row = k // 16, (k % 16) * 8
            lanes = slice(head * DIM, (head + 1) * DIM)
            for r in range(8):
                payload_ref[k, :, r * 128 : (r + 1) * 128] = state_ref[row + r : row + r + 1, lanes]
            payload_ref[k, :, ASKED:] = jnp.where(
                iota((1, 128), 1) < 64, payload_ref[k, :, ASKED:], total_ref[0:1, head : head + 1]
            )


def scan_kernel(arrived_ref, before_ref):
    carried = [jnp.zeros((1, 128), f32) for _ in range(8)]
    for k in range(OWNERS):
        decay = jnp.exp(jnp.broadcast_to(arrived_ref[k, :, PAYLOAD - 1 :], (1, 128)))
        for r in range(8):
            before_ref[k, r : r + 1, :] = carried[r]
            carried[r] = carried[r] * decay + arrived_ref[k, :, r * 128 : (r + 1) * 128]


def local_kernel(
    frames_ref, normed_ref, inflow_ref, bc_ref, log_ref, z_w_ref,
    inner_ref, gate_ref, reach_ref, means_ref,
    state_ref, total_ref,
):
    @pl.when(pl.program_id(0) == 0)
    def _():
        state_ref[...] = jnp.zeros_like(state_ref)
        total_ref[...] = jnp.zeros_like(total_ref)

    gate_ref[...] = silu(dot(normed_ref[...], z_w_ref[...]).astype(bf16).astype(f32))
    pool = jnp.where(
        iota((BLOCK // 4, BLOCK), 0) == iota((BLOCK // 4, BLOCK), 1) // 4, 0.25, 0.0
    ).astype(bf16)
    means = dot(pool, frames_ref[...])
    for g in range(4):
        means_ref[g] = means[:, g * WIDTH : (g + 1) * WIDTH]
    causal = iota((BLOCK, BLOCK), 0) >= iota((BLOCK, BLOCK), 1)
    log = log_ref[:, :HEADS]
    cum = running_sum(causal, log)
    cum_rows = filled(cum).T
    b_act, c_act = bc_ref[:, :DIM], bc_ref[:, DIM:]
    inflow = inflow_ref[...]
    scores = jnp.where(causal, lax.dot_general(c_act, b_act, NT, preferred_element_type=f32), 0.0)
    carried = dot(c_act, state_ref[...].astype(bf16)) * per_head(jnp.exp(cum))
    for h in range(HEADS):
        lanes = slice(h * DIM, (h + 1) * DIM)
        gaps = jnp.minimum(cum[:, h : h + 1] - cum_rows[h : h + 1, :], 0.0)
        mixed = (jnp.exp(gaps) * scores).astype(bf16)
        inner_ref[:, lanes] = dot(mixed, inflow[:, lanes]) + carried[:, lanes]
    reach_ref[...] = filled(jnp.exp(cum + total_ref[0:1, 0:HEADS]))
    last = cum[BLOCK - 1 :, :]
    total_ref[0:1, 0:HEADS] += last
    decayed = (inflow.astype(f32) * per_head(jnp.exp(last - cum))).astype(bf16)
    state_ref[...] = state_step(state_ref[...], decayed, cum, b_act)


def outer_kernel(
    book_ref, inner_ref, gate_ref, reach_ref, c_ref, incoming_ref, gain_ref, out_w_ref,
    out_0, out_1, out_2, out_3, pooled_ref,
):
    step = pl.program_id(0)
    pool = jnp.where(
        iota((BLOCK // 4, BLOCK), 0) == iota((BLOCK // 4, BLOCK), 1) // 4, 0.25, 0.0
    ).astype(bf16)
    c_act = c_ref[...]
    for h in range(HEADS):
        lanes = slice(h * DIM, (h + 1) * DIM)
        carried = dot(c_act, incoming_ref[lanes, :].astype(bf16))
        rows = (inner_ref[:, lanes] + carried * reach_ref[:, h : h + 1]) * gate_ref[:, lanes]
        square = jnp.mean(rows * rows, axis=1, keepdims=True)
        rows = (rows * lax.rsqrt(square + 1e-05) * gain_ref[:, lanes]).astype(bf16)
        pooled_ref[pl.ds(step * (BLOCK // 4), BLOCK // 4), lanes] = dot(pool, rows)

    @pl.when(step == STEPS - 1)
    def _():
        pooled = pooled_ref[...]
        high = pooled.astype(bf16)
        low = (pooled - high.astype(f32)).astype(bf16)
        both = jnp.concatenate([high, low], axis=0)
        for shift, out in enumerate((out_0, out_1, out_2, out_3)):
            start = pl.multiple_of(((book_ref[0] + shift) % 4) * WIDTH, WIDTH)
            product = dot(both, out_w_ref[:, pl.ds(start, WIDTH)])
            out[...] = product[:QROWS] + product[QROWS:]


def split_rows(ref, values):
    rows = values.shape[0]
    ref[pl.ds(0, rows, 2), :] = values[:, :128]
    ref[pl.ds(1, rows, 2), :] = values[:, 128:]


def lookup_kernel(cuts, arrived_ref, table_ref, *refs):
    founds, (asked_ref, columns_ref, total_ref) = refs[: len(cuts)], refs[len(cuts) :]
    level = pl.program_id(0)

    @pl.when(level == 0)
    def _():
        for k in range(OWNERS):
            asked_ref[k : k + 1, :] = arrived_ref[k, :, ASKED:]
        turned = asked_ref[...].T
        start = 0
        for low, high in cuts:
            for k in range(OWNERS):
                columns_ref[start : start + high - low, :] = jnp.broadcast_to(
                    turned[low:high, k : k + 1], (high - low, 128)
                )
                start += high - low
        total_ref[...] = jnp.zeros_like(total_ref)

    place = iota((OWNERS * SLOTS, 128), 1) + (level * CODES + 1)
    asked = columns_ref[...].astype(jnp.int32)
    chosen = jnp.concatenate(
        [(asked == place + g * 128).astype(bf16) for g in range(CODES // 128)], axis=1
    )
    total_ref[...] += dot(chosen, table_ref[0].astype(bf16))

    @pl.when(level == LEVELS - 1)
    def _():
        for (low, high), found_ref in zip(cuts, founds):
            split_rows(found_ref, total_ref[OWNERS * low : OWNERS * high, :])


def joined_rows(ref):
    half = ref.shape[0] // 2
    return jnp.concatenate([ref[pl.ds(0, half, 2), :], ref[pl.ds(1, half, 2), :]], axis=1)


def places_kernel(slots_ref, columns_ref, spreads_ref):
    total = spreads_ref.shape[0]
    slots = jnp.concatenate(
        [slots_ref[...].astype(f32), jnp.zeros((128 - LEVELS, QROWS), f32)], axis=0
    )
    columns_ref[...] = slots.T.astype(jnp.int32)
    place = iota((total, QROWS), 0)
    spread = place == slots_ref[0:1, :]
    for k in range(1, LEVELS):
        here = place == slots_ref[k : k + 1, :]
        spreads_ref[:, (k - 1) * QROWS : k * QROWS] = here.astype(bf16)
        spread = spread | here
    spreads_ref[:, (LEVELS - 1) * QROWS :] = spread.astype(bf16)


def taken_kernel(found_ref, columns_ref, spreads_ref, terms_ref, taken_ref):
    found = joined_rows(found_ref)
    rounded = found.astype(bf16)
    taken = jnp.zeros((QROWS, WIDTH), f32)
    terms = found
    for k in range(LEVELS):
        if k:
            spread = spreads_ref[:, (k - 1) * QROWS : k * QROWS]
            terms = terms + folded(dot(spread, two_parts(taken)))
        places = iota((QROWS, found.shape[0]), 1)
        picks = (columns_ref[:, k : k + 1] == places).astype(bf16)
        taken = taken + dot(picks, rounded)
    terms_ref[...] = terms
    taken_ref[...] = taken


def residual_kernel(
    book_ref, own_ref, from_1, from_2, from_3, means_ref, taken_ref, terms_ref, spread_ref,
    residual_ref, grads_ref,
):
    pooled = own_ref[...] + from_1[...] + from_2[...] + from_3[...] + means_ref[0]
    residual_ref[...] = pooled - taken_ref[...]
    grads = terms_ref[...] - folded(dot(spread_ref[...], two_parts(pooled)))
    split_rows(grads_ref, grads)


def table_kernel(codes_ref, *refs):
    grads_refs, (table_ref, rounded_ref, low_ref, high_ref) = refs[:-4], refs[-4:]
    step = pl.program_id(0)
    total = codes_ref.shape[1]

    @pl.when(step == 0)
    def _():
        start = 0
        for grads_ref in grads_refs:
            rows = grads_ref.shape[0] // 2
            rounded_ref[start : start + rows, :] = joined_rows(grads_ref).astype(bf16)
            start += rows
        code = codes_ref[...] - 1
        low_ref[...] = ((code & 127) == iota((128, total), 0)).astype(bf16)
        high_ref[...] = jnp.broadcast_to(code >> 7, (16, total))

    groups = table_ref.shape[0] // 128
    chosen = []
    for g in range(groups):
        mask = (high_ref[...] == step * groups + g).astype(bf16)
        chosen.append(low_ref[...] * jnp.concatenate([mask] * 8, axis=0))
    table_ref[...] = dot(jnp.concatenate(chosen, axis=0), rounded_ref[...])


def add_kernel(found_ref, late_ref, sum_ref):
    sum_ref[...] = found_ref[...] + late_ref[...]


def shape(*dims, dtype=f32):
    return jax.ShapeDtypeStruct(dims, dtype)


def whole(*dims):
    return pl.BlockSpec(dims, lambda *_: (0,) * len(dims))


def rows_of(rows, columns):
    return pl.BlockSpec((rows, columns), lambda i, *_: (i, 0))


def settings(mib):
    return pltpu.CompilerParams(vmem_limit_bytes=mib * 2**20)


def exchange(array):
    return lax.all_to_all(array, SEQ, split_axis=0, concat_axis=0, tiled=True)


def looked_up(arrived, codebook, cuts):
    return pl.pallas_call(
        functools.partial(lookup_kernel, cuts),
        grid=(LEVELS,),
        in_specs=[
            whole(OWNERS, 1, PAYLOAD), pl.BlockSpec((1, CODES, WIDTH), lambda i: (i, 0, 0)),
        ],
        out_specs=[whole(2 * OWNERS * (high - low), 128) for low, high in cuts],
        out_shape=[shape(2 * OWNERS * (high - low), 128) for low, high in cuts],
        scratch_shapes=[
            pltpu.VMEM((OWNERS, 128), f32), pltpu.VMEM((OWNERS * SLOTS, 128), f32),
            pltpu.VMEM((OWNERS * SLOTS, WIDTH), f32),
        ],
        compiler_params=settings(62),
        cost_estimate=pl.CostEstimate(flops=4 * 10**9, bytes_accessed=5 * 2**20, transcendentals=0),
        name="lookup",
    )(arrived, codebook)


def scanned(arrived):
    before = pl.pallas_call(
        scan_kernel,
        out_shape=shape(OWNERS, 8, 128),
        compiler_params=settings(16),
        name="scan",
    )(arrived)
    arrived, before = lax.optimization_barrier((arrived, before))
    return exchange(before).reshape(INNER, DIM), arrived


def shared_out(book, incoming, inner, gate, reach, bc_act, out_gain, out_weight):
    shares = pl.pallas_call(
        outer_kernel,
        grid_spec=pltpu.PrefetchScalarGridSpec(
            num_scalar_prefetch=1,
            grid=(STEPS,),
            in_specs=[
                rows_of(BLOCK, INNER), rows_of(BLOCK, INNER), rows_of(BLOCK, 128),
                pl.BlockSpec((BLOCK, DIM), lambda i, *_: (i, 1)),
                whole(INNER, DIM), whole(1, INNER), whole(INNER, 1024),
            ],
            out_specs=[whole(QROWS, WIDTH)] * 4,
            scratch_shapes=[pltpu.VMEM((QROWS, INNER), f32)],
        ),
        out_shape=[shape(QROWS, WIDTH)] * 4,
        compiler_params=settings(62),
        cost_estimate=pl.CostEstimate(flops=2 * 10**9, bytes_accessed=8 * 2**20, transcendentals=10**5),
        name="outer",
    )(book, inner, gate, reach, bc_act, incoming, out_gain.reshape(1, -1), out_weight)
    moved = [
        lax.ppermute(shares[d], "book", [(i, (i + d) % 4) for i in range(4)]) for d in (1, 2, 3)
    ]
    return [shares[0], *moved]


def gradient_terms(book, found, slots, shares, means):
    total = OWNERS * found.shape[1] // 2
    fetched = exchange(found)
    own, slots = lax.optimization_barrier((shares[0], slots))
    columns, spreads = pl.pallas_call(
        places_kernel,
        out_shape=[
            shape(QROWS, 128, dtype=jnp.int32), shape(total, LEVELS * QROWS, dtype=bf16),
        ],
        compiler_params=settings(32),
        cost_estimate=pl.CostEstimate(flops=10**9, bytes_accessed=2**20, transcendentals=0),
        name="places",
    )(slots)
    terms, taken = pl.pallas_call(
        taken_kernel,
        out_shape=[shape(total, WIDTH), shape(QROWS, WIDTH)],
        compiler_params=settings(24),
        cost_estimate=pl.CostEstimate(flops=3 * 10**9, bytes_accessed=3 * 2**20, transcendentals=0),
        name="taken",
    )(fetched.reshape(2 * total, 128), columns, spreads)
    residual, grads = pl.pallas_call(
        residual_kernel,
        grid_spec=pltpu.PrefetchScalarGridSpec(
            num_scalar_prefetch=1,
            grid=(1,),
            in_specs=[whole(QROWS, WIDTH)] * 4
            + [
                pl.BlockSpec((1, QROWS, WIDTH), lambda i, book: (book[0], 0, 0)),
                whole(QROWS, WIDTH), whole(total, WIDTH),
                pl.BlockSpec((total, QROWS), lambda i, book: (0, LEVELS - 1)),
            ],
            out_specs=[whole(QROWS, WIDTH), whole(2 * total, 128)],
        ),
        out_shape=[shape(QROWS, WIDTH), shape(2 * total, 128)],
        compiler_params=settings(24),
        name="residual",
    )(book, own, *shares[1:], means, taken, terms, spreads)
    return residual, grads.reshape(found.shape)


def gathered_table(codes, *grads):
    return pl.pallas_call(
        table_kernel,
        grid=(3,),
        in_specs=[whole(*codes.shape)] + [whole(*part.shape) for part in grads],
        out_specs=rows_of(CODES, WIDTH),
        out_shape=shape(LEVELS * CODES, WIDTH),
        scratch_shapes=[
            pltpu.VMEM((codes.shape[1], WIDTH), bf16), pltpu.VMEM((128, codes.shape[1]), bf16),
            pltpu.VMEM((16, codes.shape[1]), jnp.int32),
        ],
        compiler_params=settings(40),
        name="table",
    )(codes, *grads)


def asked_codes(arrived, low, high):
    return arrived[:, 0, ASKED + low : ASKED + high].astype(jnp.int32).reshape(1, -1)


def other_core(array):
    return lax.ppermute(array, "seq_2", [(0, 1), (1, 0)])


def with_all_slots(
    book, arrived, few, slots, inner, gate, reach, means, bc_act, out_gain, out_weight, codebook
):
    incoming, arrived = scanned(arrived)
    [found] = looked_up(arrived, codebook, [(0, SLOTS)])
    shares = shared_out(book, incoming, inner, gate, reach, bc_act, out_gain, out_weight)
    residual, grads = gradient_terms(
        book, found.reshape(OWNERS, 2 * SLOTS, 128), slots, shares, means
    )
    arrived, grads = lax.optimization_barrier((arrived, grads))
    returned = exchange(grads).reshape(-1, 128)
    return residual, gathered_table(asked_codes(arrived, 0, SLOTS), returned)


def with_few_slots(
    book, arrived, few, slots, inner, gate, reach, means, bc_act, out_gain, out_weight, codebook
):
    incoming, arrived = scanned(arrived)
    found, late = looked_up(arrived, codebook, [(0, FEW), (FEW, SLOTS)])
    late, incoming = lax.optimization_barrier((late, incoming))
    late = other_core(late).reshape(OWNERS, 2 * LATE, 128)
    found = found.reshape(OWNERS, 2 * FEW, 128)
    last = pl.BlockSpec((OWNERS, 2 * LATE, 128), lambda i: (0, FEW // LATE - 1, 0))
    found = pl.pallas_call(
        add_kernel,
        grid=(1,),
        in_specs=[last, whole(OWNERS, 2 * LATE, 128)],
        out_specs=last,
        out_shape=shape(OWNERS, 2 * FEW, 128),
        input_output_aliases={0: 0},
        compiler_params=settings(57),
        name="relayed",
    )(found, late)
    shares = shared_out(book, incoming, inner, gate, reach, bc_act, out_gain, out_weight)
    residual, grads = gradient_terms(book, found, few, shares, means)
    arrived, grads = lax.optimization_barrier((arrived, grads))
    codes = jnp.concatenate(
        [asked_codes(arrived, 0, FEW), asked_codes(arrived, FEW, SLOTS)], axis=1
    )
    returned, codes = lax.optimization_barrier((exchange(grads), codes))
    late = other_core(returned[:, 2 * (FEW - LATE) :].reshape(-1, 128))
    return residual, gathered_table(codes, returned.reshape(-1, 128), late)


def body(
    frames, norm_gain, x_weight, z_weight, bc_weight, dt_weight, dt_bias, decay_rate,
    out_gain, out_weight, codebook, code_ids,
):
    book = lax.axis_index("book").reshape(1)
    payload, slots, few, hot, normed, inflow, bc_act, log = pl.pallas_call(
        front_kernel,
        grid=(STEPS,),
        in_specs=[
            rows_of(BLOCK, 1024), whole(1, 1024), whole(1024, INNER), whole(1024, 256),
            whole(HEADS, 1024), whole(1, HEADS), whole(1, HEADS), whole(LEVELS, QROWS),
        ],
        out_specs=[
            whole(OWNERS, 1, PAYLOAD), whole(LEVELS, QROWS), whole(LEVELS, QROWS),
            whole(1, 128), rows_of(BLOCK, 1024),
            rows_of(BLOCK, INNER), rows_of(BLOCK, 256), rows_of(BLOCK, 128),
        ],
        out_shape=[
            shape(OWNERS, 1, PAYLOAD), shape(LEVELS, QROWS, dtype=jnp.int32),
            shape(LEVELS, QROWS, dtype=jnp.int32), shape(1, 128),
            shape(FRAMES, 1024, dtype=bf16), shape(FRAMES, INNER, dtype=bf16),
            shape(FRAMES, 256, dtype=bf16), shape(FRAMES, 128),
        ],
        scratch_shapes=[pltpu.VMEM((DIM, INNER), f32), pltpu.VMEM((8, 128), f32)],
        compiler_params=settings(62),
        name="front",
    )(
        frames, norm_gain.reshape(1, -1), x_weight, bc_weight, dt_weight.T,
        dt_bias.reshape(1, -1), decay_rate.reshape(1, -1), code_ids,
    )
    arrived = exchange(payload)
    inner, gate, reach, means = pl.pallas_call(
        local_kernel,
        grid=(STEPS,),
        in_specs=[
            rows_of(BLOCK, 1024), rows_of(BLOCK, 1024), rows_of(BLOCK, INNER),
            rows_of(BLOCK, 256), rows_of(BLOCK, 128), whole(1024, INNER),
        ],
        out_specs=[
            rows_of(BLOCK, INNER), rows_of(BLOCK, INNER), rows_of(BLOCK, 128),
            pl.BlockSpec((4, BLOCK // 4, WIDTH), lambda i: (0, i, 0)),
        ],
        out_shape=[
            shape(FRAMES, INNER), shape(FRAMES, INNER), shape(FRAMES, 128),
            shape(4, QROWS, WIDTH),
        ],
        scratch_shapes=[pltpu.VMEM((DIM, INNER), f32), pltpu.VMEM((8, 128), f32)],
        compiler_params=settings(62),
        cost_estimate=pl.CostEstimate(flops=4 * 10**9, bytes_accessed=12 * 2**20, transcendentals=10**6),
        name="local",
    )(frames, normed, inflow, bc_act, log, z_weight)
    arrived, inner = lax.optimization_barrier((arrived, inner))
    residual, table = lax.cond(
        hot[0, 0] < 1.5, with_few_slots, with_all_slots,
        book, arrived, few, slots, inner, gate, reach, means, bc_act, out_gain, out_weight, codebook,
    )
    return residual, table.reshape(LEVELS, CODES, WIDTH)


def solution(mesh):
    finer = Mesh(
        mesh.devices.reshape(8, 4, 2, mesh.shape["book"]), ("seq_0", "seq_1", "seq_2", "book")
    )
    placed = (
        P(SEQ, None), P(), P(None, "book"), P(None, "book"), P(), P(None, "book"), P("book"),
        P("book"), P("book"), P("book", None), P(None, SEQ, "book"), P(None, SEQ),
    )
    return jax.shard_map(
        body,
        mesh=finer,
        in_specs=placed,
        out_specs=(P(SEQ, "book"), P(None, SEQ, "book")),
        check_vma=False,
    )
```

```python
import functools

import jax
import jax.numpy as jnp
from jax import lax
from jax.experimental import pallas as pl
from jax.experimental.pallas import tpu as pltpu
from jax.sharding import Mesh
from jax.sharding import PartitionSpec as P

SEQ = ("seq_0", "seq_1", "seq_2")
OWNERS = 64
SLOTS = 20
FEW = 16
LATE = SLOTS - FEW
LEVELS = 3
LOW = 4
CODES = 1024
FRAMES = 1024
BLOCK = 256
STEPS = FRAMES // BLOCK
QROWS = 256
WIDTH = 256
HEADS = 4
DIM = 128
INNER = HEADS * DIM
PAYLOAD = 9 * 128
ASKED = 8 * 128

f32 = jnp.float32
bf16 = jnp.bfloat16
HIGHEST = lax.Precision.HIGHEST
NT = (((1,), (1,)), ((), ()))


def dot(a, b):
    return jnp.dot(a, b, preferred_element_type=f32)


def three_parts(values):
    high = values.astype(bf16)
    rest = values - high.astype(f32)
    middle = rest.astype(bf16)
    return high, middle, (rest - middle.astype(f32)).astype(bf16)


def iota(shape, dim):
    return lax.broadcasted_iota(jnp.int32, shape, dim)


def two_parts(values):
    high = values.astype(bf16)
    low = (values - high.astype(f32)).astype(bf16)
    return jnp.concatenate([high, low], axis=1)


def folded(values):
    half = values.shape[1] // 2
    return values[:, :half] + values[:, half:]


def silu(values):
    return values * jax.nn.sigmoid(values)


def filled(columns):
    return jnp.concatenate([columns, jnp.zeros((columns.shape[0], 128 - HEADS), f32)], axis=1)


def per_head(columns):
    rows = columns.shape[0]
    return jnp.concatenate(
        [jnp.broadcast_to(columns[:, h : h + 1], (rows, DIM)) for h in range(HEADS)], axis=1
    )


def running_sum(causal, values):
    ones = causal.astype(bf16)
    return sum(dot(ones, part) for part in three_parts(values))


def state_step(state, decayed, cum, b_act):
    return state * per_head(jnp.exp(cum[BLOCK - 1 :, :])) + dot(b_act.T, decayed)


def place_codes(ids_ref, slots_ref, few_ref, hot_ref):
    entries = LEVELS * QROWS
    ids = jnp.concatenate([ids_ref[k : k + 1, :] for k in range(LEVELS)], axis=1)
    level = iota((1, entries), 1) // QROWS
    owner = ids // CODES
    wanted = level * CODES + ids % CODES + 1
    member = (iota((OWNERS, entries), 0) == owner).astype(f32)
    before = (iota((QROWS, QROWS), 0) < iota((QROWS, QROWS), 1)).astype(bf16)
    seen = jnp.zeros((OWNERS, 1), f32)
    hot = jnp.zeros((OWNERS, 1), f32)
    ranks = []
    for k in range(LEVELS):
        part = member[:, k * QROWS : (k + 1) * QROWS]
        ranks.append(jnp.sum(part * (dot(part.astype(bf16), before) + seen), axis=0, keepdims=True))
        count = jnp.sum(part, axis=1, keepdims=True)
        seen = seen + count
        hot = jnp.maximum(hot, jnp.where(count > LOW, 1.0, 0.0))
    rank = jnp.concatenate(ranks, axis=1).astype(jnp.int32)
    slot = owner * SLOTS + rank
    neighbour = owner + 1 - 2 * (owner % 2)
    few = jnp.where(rank < FEW, owner * FEW + rank, neighbour * FEW + rank - LATE)
    for k in range(LEVELS):
        slots_ref[k : k + 1, :] = slot[:, k * QROWS : (k + 1) * QROWS]
        few_ref[k : k + 1, :] = few[:, k * QROWS : (k + 1) * QROWS]
    chip = (iota((OWNERS // 2, OWNERS), 0) == iota((OWNERS // 2, OWNERS), 1) // 2).astype(bf16)
    on_chip = dot(chip, jnp.broadcast_to(hot, (OWNERS, 128)).astype(bf16))
    hot_ref[...] = jnp.max(on_chip, axis=0, keepdims=True)
    ranked = (iota((128, entries), 0) == rank).astype(bf16)
    high = (member * (wanted // 64).astype(f32)).astype(bf16)
    low = (member * (wanted % 64).astype(f32)).astype(bf16)
    return 64.0 * lax.dot_general(high, ranked, NT, preferred_element_type=f32) + lax.dot_general(
        low, ranked, NT, preferred_element_type=f32
    )


def front_kernel(
    frames_ref, gain_ref, x_w_ref, bc_w_ref, dt_w_ref, bias_ref, rate_ref, ids_ref,
    payload_ref, slots_ref, few_ref, hot_ref, normed_ref, inflow_ref, bc_ref, log_ref,
    state_ref, total_ref,
):
    step = pl.program_id(0)

    @pl.when(step == 0)
    def _():
        state_ref[...] = jnp.zeros_like(state_ref)
        total_ref[...] = jnp.zeros_like(total_ref)
        asked = place_codes(ids_ref, slots_ref, few_ref, hot_ref)
        for k in range(OWNERS):
            payload_ref[k, :, ASKED:] = asked[k : k + 1, :]

    frames = frames_ref[...].astype(f32)
    square = jnp.mean(frames * frames, axis=1, keepdims=True)
    normed = (frames * lax.rsqrt(square + 1e-05) * gain_ref[...]).astype(bf16)
    normed_ref[...] = normed
    bc_act = silu(dot(normed, bc_w_ref[...]).astype(bf16).astype(f32)).astype(bf16)
    bc_ref[...] = bc_act
    raw = lax.dot_general(normed, dt_w_ref[...], NT, preferred_element_type=f32) + bias_ref[...]
    dt = jnp.maximum(raw, 0.0) + jnp.log1p(jnp.exp(-jnp.abs(raw)))
    log = -dt * rate_ref[...]
    log_ref[...] = filled(log)
    causal = iota((BLOCK, BLOCK), 0) >= iota((BLOCK, BLOCK), 1)
    cum = running_sum(causal, log)
    x_act = silu(dot(normed, x_w_ref[...]).astype(bf16).astype(f32))
    inflow = x_act * per_head(dt)
    inflow_ref[...] = inflow.astype(bf16)
    last = cum[BLOCK - 1 :, :]
    decayed = (inflow * per_head(jnp.exp(last - cum))).astype(bf16)
    state_ref[...] = state_step(state_ref[...], decayed, cum, bc_act[:, :DIM])
    total_ref[0:1, 0:HEADS] += last

    @pl.when(step == STEPS - 1)
    def _():
        for k in range(OWNERS):
            head, row = k // 16, (k % 16) * 8
            lanes = slice(head * DIM, (head + 1) * DIM)
            for r in range(8):
                payload_ref[k, :, r * 128 : (r + 1) * 128] = state_ref[row + r : row + r + 1, lanes]
            payload_ref[k, :, ASKED:] = jnp.where(
                iota((1, 128), 1) < 64, payload_ref[k, :, ASKED:], total_ref[0:1, head : head + 1]
            )


def scan_kernel(arrived_ref, before_ref):
    carried = [jnp.zeros((1, 128), f32) for _ in range(8)]
    for k in range(OWNERS):
        decay = jnp.exp(jnp.broadcast_to(arrived_ref[k, :, PAYLOAD - 1 :], (1, 128)))
        for r in range(8):
            before_ref[k, r : r + 1, :] = carried[r]
            carried[r] = carried[r] * decay + arrived_ref[k, :, r * 128 : (r + 1) * 128]


def local_kernel(
    frames_ref, normed_ref, inflow_ref, bc_ref, log_ref, z_w_ref,
    inner_ref, gate_ref, reach_ref, means_ref,
    state_ref, total_ref,
):
    @pl.when(pl.program_id(0) == 0)
    def _():
        state_ref[...] = jnp.zeros_like(state_ref)
        total_ref[...] = jnp.zeros_like(total_ref)

    gate_ref[...] = silu(dot(normed_ref[...], z_w_ref[...]).astype(bf16).astype(f32))
    pool = jnp.where(
        iota((BLOCK // 4, BLOCK), 0) == iota((BLOCK // 4, BLOCK), 1) // 4, 0.25, 0.0
    ).astype(bf16)
    means = dot(pool, frames_ref[...])
    for g in range(4):
        means_ref[g] = means[:, g * WIDTH : (g + 1) * WIDTH]
    causal = iota((BLOCK, BLOCK), 0) >= iota((BLOCK, BLOCK), 1)
    log = log_ref[:, :HEADS]
    cum = running_sum(causal, log)
    cum_rows = filled(cum).T
    b_act, c_act = bc_ref[:, :DIM], bc_ref[:, DIM:]
    inflow = inflow_ref[...]
    scores = jnp.where(causal, lax.dot_general(c_act, b_act, NT, preferred_element_type=f32), 0.0)
    carried = dot(c_act, state_ref[...].astype(bf16)) * per_head(jnp.exp(cum))
    for h in range(HEADS):
        lanes = slice(h * DIM, (h + 1) * DIM)
        gaps = jnp.minimum(cum[:, h : h + 1] - cum_rows[h : h + 1, :], 0.0)
        mixed = (jnp.exp(gaps) * scores).astype(bf16)
        inner_ref[:, lanes] = dot(mixed, inflow[:, lanes]) + carried[:, lanes]
    reach_ref[...] = filled(jnp.exp(cum + total_ref[0:1, 0:HEADS]))
    last = cum[BLOCK - 1 :, :]
    total_ref[0:1, 0:HEADS] += last
    decayed = (inflow.astype(f32) * per_head(jnp.exp(last - cum))).astype(bf16)
    state_ref[...] = state_step(state_ref[...], decayed, cum, b_act)


def outer_kernel(
    book_ref, inner_ref, gate_ref, reach_ref, c_ref, incoming_ref, gain_ref, out_w_ref,
    out_0, out_1, out_2, out_3, pooled_ref,
):
    step = pl.program_id(0)
    pool = jnp.where(
        iota((BLOCK // 4, BLOCK), 0) == iota((BLOCK // 4, BLOCK), 1) // 4, 0.25, 0.0
    ).astype(bf16)
    c_act = c_ref[...]
    for h in range(HEADS):
        lanes = slice(h * DIM, (h + 1) * DIM)
        carried = dot(c_act, incoming_ref[lanes, :].astype(bf16))
        rows = (inner_ref[:, lanes] + carried * reach_ref[:, h : h + 1]) * gate_ref[:, lanes]
        square = jnp.mean(rows * rows, axis=1, keepdims=True)
        rows = (rows * lax.rsqrt(square + 1e-05) * gain_ref[:, lanes]).astype(bf16)
        pooled_ref[pl.ds(step * (BLOCK // 4), BLOCK // 4), lanes] = dot(pool, rows)

    @pl.when(step == STEPS - 1)
    def _():
        pooled = pooled_ref[...]
        high = pooled.astype(bf16)
        low = (pooled - high.astype(f32)).astype(bf16)
        both = jnp.concatenate([high, low], axis=0)
        for shift, out in enumerate((out_0, out_1, out_2, out_3)):
            start = pl.multiple_of(((book_ref[0] + shift) % 4) * WIDTH, WIDTH)
            product = dot(both, out_w_ref[:, pl.ds(start, WIDTH)])
            out[...] = product[:QROWS] + product[QROWS:]


def split_rows(ref, values):
    rows = values.shape[0]
    ref[pl.ds(0, rows, 2), :] = values[:, :128]
    ref[pl.ds(1, rows, 2), :] = values[:, 128:]


def lookup_kernel(cuts, arrived_ref, table_ref, *refs):
    founds, (asked_ref, columns_ref, total_ref) = refs[: len(cuts)], refs[len(cuts) :]
    level = pl.program_id(0)

    @pl.when(level == 0)
    def _():
        for k in range(OWNERS):
            asked_ref[k : k + 1, :] = arrived_ref[k, :, ASKED:]
        turned = asked_ref[...].T
        start = 0
        for low, high in cuts:
            for k in range(OWNERS):
                columns_ref[start : start + high - low, :] = jnp.broadcast_to(
                    turned[low:high, k : k + 1], (high - low, 128)
                )
                start += high - low
        total_ref[...] = jnp.zeros_like(total_ref)

    place = iota((OWNERS * SLOTS, 128), 1) + (level * CODES + 1)
    asked = columns_ref[...].astype(jnp.int32)
    chosen = jnp.concatenate(
        [(asked == place + g * 128).astype(bf16) for g in range(CODES // 128)], axis=1
    )
    total_ref[...] += dot(chosen, table_ref[0].astype(bf16))

    @pl.when(level == LEVELS - 1)
    def _():
        for (low, high), found_ref in zip(cuts, founds):
            split_rows(found_ref, total_ref[OWNERS * low : OWNERS * high, :])


def joined_rows(ref):
    half = ref.shape[0] // 2
    return jnp.concatenate([ref[pl.ds(0, half, 2), :], ref[pl.ds(1, half, 2), :]], axis=1)


def places_kernel(slots_ref, columns_ref, spreads_ref):
    total = spreads_ref.shape[0]
    slots = jnp.concatenate(
        [slots_ref[...].astype(f32), jnp.zeros((128 - LEVELS, QROWS), f32)], axis=0
    )
    columns_ref[...] = slots.T.astype(jnp.int32)
    place = iota((total, QROWS), 0)
    spread = place == slots_ref[0:1, :]
    for k in range(1, LEVELS):
        here = place == slots_ref[k : k + 1, :]
        spreads_ref[:, (k - 1) * QROWS : k * QROWS] = here.astype(bf16)
        spread = spread | here
    spreads_ref[:, (LEVELS - 1) * QROWS :] = spread.astype(bf16)


def taken_kernel(found_ref, columns_ref, spreads_ref, terms_ref, taken_ref):
    found = joined_rows(found_ref)
    rounded = found.astype(bf16)
    taken = jnp.zeros((QROWS, WIDTH), f32)
    terms = found
    for k in range(LEVELS):
        if k:
            spread = spreads_ref[:, (k - 1) * QROWS : k * QROWS]
            terms = terms + folded(dot(spread, two_parts(taken)))
        places = iota((QROWS, found.shape[0]), 1)
        picks = (columns_ref[:, k : k + 1] == places).astype(bf16)
        taken = taken + dot(picks, rounded)
    terms_ref[...] = terms
    taken_ref[...] = taken


def residual_kernel(
    book_ref, own_ref, from_1, from_2, from_3, means_ref, taken_ref, terms_ref, spread_ref,
    residual_ref, grads_ref,
):
    pooled = own_ref[...] + from_1[...] + from_2[...] + from_3[...] + means_ref[0]
    residual_ref[...] = pooled - taken_ref[...]
    grads = terms_ref[...] - folded(dot(spread_ref[...], two_parts(pooled)))
    split_rows(grads_ref, grads)


def table_kernel(codes_ref, *refs):
    grads_refs, (table_ref, rounded_ref, low_ref, high_ref) = refs[:-4], refs[-4:]
    step = pl.program_id(0)
    total = codes_ref.shape[1]

    @pl.when(step == 0)
    def _():
        start = 0
        for grads_ref in grads_refs:
            rows = grads_ref.shape[0] // 2
            rounded_ref[start : start + rows, :] = joined_rows(grads_ref).astype(bf16)
            start += rows
        code = codes_ref[...] - 1
        low_ref[...] = ((code & 127) == iota((128, total), 0)).astype(bf16)
        high_ref[...] = jnp.broadcast_to(code >> 7, (16, total))

    groups = table_ref.shape[0] // 128
    chosen = []
    for g in range(groups):
        mask = (high_ref[...] == step * groups + g).astype(bf16)
        chosen.append(low_ref[...] * jnp.concatenate([mask] * 8, axis=0))
    table_ref[...] = dot(jnp.concatenate(chosen, axis=0), rounded_ref[...])


def add_kernel(found_ref, late_ref, sum_ref):
    sum_ref[...] = found_ref[...] + late_ref[...]


def shape(*dims, dtype=f32):
    return jax.ShapeDtypeStruct(dims, dtype)


def whole(*dims):
    return pl.BlockSpec(dims, lambda *_: (0,) * len(dims))


def rows_of(rows, columns):
    return pl.BlockSpec((rows, columns), lambda i, *_: (i, 0))


def settings(mib):
    return pltpu.CompilerParams(vmem_limit_bytes=mib * 2**20)


def exchange(array):
    return lax.all_to_all(array, SEQ, split_axis=0, concat_axis=0, tiled=True)


def looked_up(arrived, codebook, cuts):
    return pl.pallas_call(
        functools.partial(lookup_kernel, cuts),
        grid=(LEVELS,),
        in_specs=[
            whole(OWNERS, 1, PAYLOAD), pl.BlockSpec((1, CODES, WIDTH), lambda i: (i, 0, 0)),
        ],
        out_specs=[whole(2 * OWNERS * (high - low), 128) for low, high in cuts],
        out_shape=[shape(2 * OWNERS * (high - low), 128) for low, high in cuts],
        scratch_shapes=[
            pltpu.VMEM((OWNERS, 128), f32), pltpu.VMEM((OWNERS * SLOTS, 128), f32),
            pltpu.VMEM((OWNERS * SLOTS, WIDTH), f32),
        ],
        compiler_params=settings(62),
        cost_estimate=pl.CostEstimate(flops=4 * 10**9, bytes_accessed=5 * 2**20, transcendentals=0),
        name="lookup",
    )(arrived, codebook)


def scanned(arrived):
    before = pl.pallas_call(
        scan_kernel,
        out_shape=shape(OWNERS, 8, 128),
        compiler_params=settings(16),
        name="scan",
    )(arrived)
    arrived, before = lax.optimization_barrier((arrived, before))
    return exchange(before).reshape(INNER, DIM), arrived


def shared_out(book, incoming, inner, gate, reach, bc_act, out_gain, out_weight):
    shares = pl.pallas_call(
        outer_kernel,
        grid_spec=pltpu.PrefetchScalarGridSpec(
            num_scalar_prefetch=1,
            grid=(STEPS,),
            in_specs=[
                rows_of(BLOCK, INNER), rows_of(BLOCK, INNER), rows_of(BLOCK, 128),
                pl.BlockSpec((BLOCK, DIM), lambda i, *_: (i, 1)),
                whole(INNER, DIM), whole(1, INNER), whole(INNER, 1024),
            ],
            out_specs=[whole(QROWS, WIDTH)] * 4,
            scratch_shapes=[pltpu.VMEM((QROWS, INNER), f32)],
        ),
        out_shape=[shape(QROWS, WIDTH)] * 4,
        compiler_params=settings(62),
        cost_estimate=pl.CostEstimate(flops=2 * 10**9, bytes_accessed=8 * 2**20, transcendentals=10**5),
        name="outer",
    )(book, inner, gate, reach, bc_act, incoming, out_gain.reshape(1, -1), out_weight)
    moved = [
        lax.ppermute(shares[d], "book", [(i, (i + d) % 4) for i in range(4)]) for d in (1, 2, 3)
    ]
    return [shares[0], *moved]


def gradient_terms(book, found, slots, shares, means):
    total = OWNERS * found.shape[1] // 2
    fetched = exchange(found)
    own, slots = lax.optimization_barrier((shares[0], slots))
    columns, spreads = pl.pallas_call(
        places_kernel,
        out_shape=[
            shape(QROWS, 128, dtype=jnp.int32), shape(total, LEVELS * QROWS, dtype=bf16),
        ],
        compiler_params=settings(32),
        cost_estimate=pl.CostEstimate(flops=10**9, bytes_accessed=2**20, transcendentals=0),
        name="places",
    )(slots)
    terms, taken = pl.pallas_call(
        taken_kernel,
        out_shape=[shape(total, WIDTH), shape(QROWS, WIDTH)],
        compiler_params=settings(24),
        cost_estimate=pl.CostEstimate(flops=3 * 10**9, bytes_accessed=3 * 2**20, transcendentals=0),
        name="taken",
    )(fetched.reshape(2 * total, 128), columns, spreads)
    residual, grads = pl.pallas_call(
        residual_kernel,
        grid_spec=pltpu.PrefetchScalarGridSpec(
            num_scalar_prefetch=1,
            grid=(1,),
            in_specs=[whole(QROWS, WIDTH)] * 4
            + [
                pl.BlockSpec((1, QROWS, WIDTH), lambda i, book: (book[0], 0, 0)),
                whole(QROWS, WIDTH), whole(total, WIDTH),
                pl.BlockSpec((total, QROWS), lambda i, book: (0, LEVELS - 1)),
            ],
            out_specs=[whole(QROWS, WIDTH), whole(2 * total, 128)],
        ),
        out_shape=[shape(QROWS, WIDTH), shape(2 * total, 128)],
        compiler_params=settings(24),
        name="residual",
    )(book, own, *shares[1:], means, taken, terms, spreads)
    return residual, grads.reshape(found.shape)


def gathered_table(codes, *grads):
    return pl.pallas_call(
        table_kernel,
        grid=(3,),
        in_specs=[whole(*codes.shape)] + [whole(*part.shape) for part in grads],
        out_specs=rows_of(CODES, WIDTH),
        out_shape=shape(LEVELS * CODES, WIDTH),
        scratch_shapes=[
            pltpu.VMEM((codes.shape[1], WIDTH), bf16), pltpu.VMEM((128, codes.shape[1]), bf16),
            pltpu.VMEM((16, codes.shape[1]), jnp.int32),
        ],
        compiler_params=settings(40),
        name="table",
    )(codes, *grads)


def asked_codes(arrived, low, high):
    return arrived[:, 0, ASKED + low : ASKED + high].astype(jnp.int32).reshape(1, -1)


def other_core(array):
    return lax.ppermute(array, "seq_2", [(0, 1), (1, 0)])


def with_all_slots(
    book, arrived, few, slots, inner, gate, reach, means, bc_act, out_gain, out_weight, codebook
):
    incoming, arrived = scanned(arrived)
    [found] = looked_up(arrived, codebook, [(0, SLOTS)])
    shares = shared_out(book, incoming, inner, gate, reach, bc_act, out_gain, out_weight)
    residual, grads = gradient_terms(
        book, found.reshape(OWNERS, 2 * SLOTS, 128), slots, shares, means
    )
    arrived, grads = lax.optimization_barrier((arrived, grads))
    returned = exchange(grads).reshape(-1, 128)
    return residual, gathered_table(asked_codes(arrived, 0, SLOTS), returned)


def with_few_slots(
    book, arrived, few, slots, inner, gate, reach, means, bc_act, out_gain, out_weight, codebook
):
    incoming, arrived = scanned(arrived)
    found, late = looked_up(arrived, codebook, [(0, FEW), (FEW, SLOTS)])
    late = other_core(late).reshape(OWNERS, 2 * LATE, 128)
    found = found.reshape(OWNERS, 2 * FEW, 128)
    last = pl.BlockSpec((OWNERS, 2 * LATE, 128), lambda i: (0, FEW // LATE - 1, 0))
    found = pl.pallas_call(
        add_kernel,
        grid=(1,),
        in_specs=[last, whole(OWNERS, 2 * LATE, 128)],
        out_specs=last,
        out_shape=shape(OWNERS, 2 * FEW, 128),
        input_output_aliases={0: 0},
        compiler_params=settings(57),
        cost_estimate=pl.CostEstimate(flops=0, bytes_accessed=0, transcendentals=0),
        name="relayed",
    )(found, late)
    shares = shared_out(book, incoming, inner, gate, reach, bc_act, out_gain, out_weight)
    residual, grads = gradient_terms(book, found, few, shares, means)
    arrived, grads = lax.optimization_barrier((arrived, grads))
    codes = jnp.concatenate(
        [asked_codes(arrived, 0, FEW), asked_codes(arrived, FEW, SLOTS)], axis=1
    )
    returned, codes = lax.optimization_barrier((exchange(grads), codes))
    late = other_core(returned[:, 2 * (FEW - LATE) :].reshape(-1, 128))
    return residual, gathered_table(codes, returned.reshape(-1, 128), late)


def body(
    frames, norm_gain, x_weight, z_weight, bc_weight, dt_weight, dt_bias, decay_rate,
    out_gain, out_weight, codebook, code_ids,
):
    book = lax.axis_index("book").reshape(1)
    payload, slots, few, hot, normed, inflow, bc_act, log = pl.pallas_call(
        front_kernel,
        grid=(STEPS,),
        in_specs=[
            rows_of(BLOCK, 1024), whole(1, 1024), whole(1024, INNER), whole(1024, 256),
            whole(HEADS, 1024), whole(1, HEADS), whole(1, HEADS), whole(LEVELS, QROWS),
        ],
        out_specs=[
            whole(OWNERS, 1, PAYLOAD), whole(LEVELS, QROWS), whole(LEVELS, QROWS),
            whole(1, 128), rows_of(BLOCK, 1024),
            rows_of(BLOCK, INNER), rows_of(BLOCK, 256), rows_of(BLOCK, 128),
        ],
        out_shape=[
            shape(OWNERS, 1, PAYLOAD), shape(LEVELS, QROWS, dtype=jnp.int32),
            shape(LEVELS, QROWS, dtype=jnp.int32), shape(1, 128),
            shape(FRAMES, 1024, dtype=bf16), shape(FRAMES, INNER, dtype=bf16),
            shape(FRAMES, 256, dtype=bf16), shape(FRAMES, 128),
        ],
        scratch_shapes=[pltpu.VMEM((DIM, INNER), f32), pltpu.VMEM((8, 128), f32)],
        compiler_params=settings(62),
        name="front",
    )(
        frames, norm_gain.reshape(1, -1), x_weight, bc_weight, dt_weight.T,
        dt_bias.reshape(1, -1), decay_rate.reshape(1, -1), code_ids,
    )
    arrived = exchange(payload)
    inner, gate, reach, means = pl.pallas_call(
        local_kernel,
        grid=(STEPS,),
        in_specs=[
            rows_of(BLOCK, 1024), rows_of(BLOCK, 1024), rows_of(BLOCK, INNER),
            rows_of(BLOCK, 256), rows_of(BLOCK, 128), whole(1024, INNER),
        ],
        out_specs=[
            rows_of(BLOCK, INNER), rows_of(BLOCK, INNER), rows_of(BLOCK, 128),
            pl.BlockSpec((4, BLOCK // 4, WIDTH), lambda i: (0, i, 0)),
        ],
        out_shape=[
            shape(FRAMES, INNER), shape(FRAMES, INNER), shape(FRAMES, 128),
            shape(4, QROWS, WIDTH),
        ],
        scratch_shapes=[pltpu.VMEM((DIM, INNER), f32), pltpu.VMEM((8, 128), f32)],
        compiler_params=settings(62),
        cost_estimate=pl.CostEstimate(flops=4 * 10**9, bytes_accessed=12 * 2**20, transcendentals=10**6),
        name="local",
    )(frames, normed, inflow, bc_act, log, z_weight)
    arrived, inner = lax.optimization_barrier((arrived, inner))
    residual, table = lax.cond(
        hot[0, 0] < 1.5, with_few_slots, with_all_slots,
        book, arrived, few, slots, inner, gate, reach, means, bc_act, out_gain, out_weight, codebook,
    )
    return residual, table.reshape(LEVELS, CODES, WIDTH)


def solution(mesh):
    finer = Mesh(
        mesh.devices.reshape(8, 4, 2, mesh.shape["book"]), ("seq_0", "seq_1", "seq_2", "book")
    )
    placed = (
        P(SEQ, None), P(), P(None, "book"), P(None, "book"), P(), P(None, "book"), P("book"),
        P("book"), P("book"), P("book", None), P(None, SEQ, "book"), P(None, SEQ),
    )
    return jax.shard_map(
        body,
        mesh=finer,
        in_specs=placed,
        out_specs=(P(SEQ, "book"), P(None, SEQ, "book")),
        check_vma=False,
    )
```

```python
import functools

import jax
import jax.numpy as jnp
from jax import lax
from jax.experimental import pallas as pl
from jax.experimental.pallas import tpu as pltpu
from jax.sharding import Mesh
from jax.sharding import PartitionSpec as P

SEQ = ("seq_0", "seq_1", "seq_2")
OWNERS = 64
SLOTS = 20
FEW = 16
LATE = SLOTS - FEW
LEVELS = 3
LOW = 4
CODES = 1024
FRAMES = 1024
BLOCK = 256
STEPS = FRAMES // BLOCK
QROWS = 256
WIDTH = 256
HEADS = 4
DIM = 128
INNER = HEADS * DIM
PAYLOAD = 9 * 128
ASKED = 8 * 128

f32 = jnp.float32
bf16 = jnp.bfloat16
HIGHEST = lax.Precision.HIGHEST
NT = (((1,), (1,)), ((), ()))


def dot(a, b):
    return jnp.dot(a, b, preferred_element_type=f32)


def three_parts(values):
    high = values.astype(bf16)
    rest = values - high.astype(f32)
    middle = rest.astype(bf16)
    return high, middle, (rest - middle.astype(f32)).astype(bf16)


def iota(shape, dim):
    return lax.broadcasted_iota(jnp.int32, shape, dim)


def two_parts(values):
    high = values.astype(bf16)
    low = (values - high.astype(f32)).astype(bf16)
    return jnp.concatenate([high, low], axis=1)


def folded(values):
    half = values.shape[1] // 2
    return values[:, :half] + values[:, half:]


def silu(values):
    return values * jax.nn.sigmoid(values)


def filled(columns):
    return jnp.concatenate([columns, jnp.zeros((columns.shape[0], 128 - HEADS), f32)], axis=1)


def per_head(columns):
    rows = columns.shape[0]
    return jnp.concatenate(
        [jnp.broadcast_to(columns[:, h : h + 1], (rows, DIM)) for h in range(HEADS)], axis=1
    )


def running_sum(causal, values):
    ones = causal.astype(bf16)
    return sum(dot(ones, part) for part in three_parts(values))


def state_step(state, decayed, cum, b_act):
    return state * per_head(jnp.exp(cum[BLOCK - 1 :, :])) + dot(b_act.T, decayed)


def place_codes(ids_ref, slots_ref, few_ref, hot_ref):
    entries = LEVELS * QROWS
    ids = jnp.concatenate([ids_ref[k : k + 1, :] for k in range(LEVELS)], axis=1)
    level = iota((1, entries), 1) // QROWS
    owner = ids // CODES
    wanted = level * CODES + ids % CODES + 1
    member = (iota((OWNERS, entries), 0) == owner).astype(f32)
    before = (iota((QROWS, QROWS), 0) < iota((QROWS, QROWS), 1)).astype(bf16)
    seen = jnp.zeros((OWNERS, 1), f32)
    hot = jnp.zeros((OWNERS, 1), f32)
    ranks = []
    for k in range(LEVELS):
        part = member[:, k * QROWS : (k + 1) * QROWS]
        ranks.append(jnp.sum(part * (dot(part.astype(bf16), before) + seen), axis=0, keepdims=True))
        count = jnp.sum(part, axis=1, keepdims=True)
        seen = seen + count
        hot = jnp.maximum(hot, jnp.where(count > LOW, 1.0, 0.0))
    rank = jnp.concatenate(ranks, axis=1).astype(jnp.int32)
    slot = owner * SLOTS + rank
    neighbour = owner + 1 - 2 * (owner % 2)
    few = jnp.where(rank < FEW, owner * FEW + rank, neighbour * FEW + rank - LATE)
    for k in range(LEVELS):
        slots_ref[k : k + 1, :] = slot[:, k * QROWS : (k + 1) * QROWS]
        few_ref[k : k + 1, :] = few[:, k * QROWS : (k + 1) * QROWS]
    chip = (iota((OWNERS // 2, OWNERS), 0) == iota((OWNERS // 2, OWNERS), 1) // 2).astype(bf16)
    on_chip = dot(chip, jnp.broadcast_to(hot, (OWNERS, 128)).astype(bf16))
    hot_ref[...] = jnp.max(on_chip, axis=0, keepdims=True)
    ranked = (iota((128, entries), 0) == rank).astype(bf16)
    high = (member * (wanted // 64).astype(f32)).astype(bf16)
    low = (member * (wanted % 64).astype(f32)).astype(bf16)
    return 64.0 * lax.dot_general(high, ranked, NT, preferred_element_type=f32) + lax.dot_general(
        low, ranked, NT, preferred_element_type=f32
    )


def front_kernel(
    frames_ref, gain_ref, x_w_ref, bc_w_ref, dt_w_ref, bias_ref, rate_ref, ids_ref,
    payload_ref, slots_ref, few_ref, hot_ref, normed_ref, inflow_ref, bc_ref, log_ref,
    state_ref, total_ref,
):
    step = pl.program_id(0)

    @pl.when(step == 0)
    def _():
        state_ref[...] = jnp.zeros_like(state_ref)
        total_ref[...] = jnp.zeros_like(total_ref)
        asked = place_codes(ids_ref, slots_ref, few_ref, hot_ref)
        for k in range(OWNERS):
            payload_ref[k, :, ASKED:] = asked[k : k + 1, :]

    frames = frames_ref[...].astype(f32)
    square = jnp.mean(frames * frames, axis=1, keepdims=True)
    normed = (frames * lax.rsqrt(square + 1e-05) * gain_ref[...]).astype(bf16)
    normed_ref[...] = normed
    bc_act = silu(dot(normed, bc_w_ref[...]).astype(bf16).astype(f32)).astype(bf16)
    bc_ref[...] = bc_act
    raw = lax.dot_general(normed, dt_w_ref[...], NT, preferred_element_type=f32) + bias_ref[...]
    dt = jnp.maximum(raw, 0.0) + jnp.log1p(jnp.exp(-jnp.abs(raw)))
    log = -dt * rate_ref[...]
    log_ref[...] = filled(log)
    causal = iota((BLOCK, BLOCK), 0) >= iota((BLOCK, BLOCK), 1)
    cum = running_sum(causal, log)
    x_act = silu(dot(normed, x_w_ref[...]).astype(bf16).astype(f32))
    inflow = x_act * per_head(dt)
    inflow_ref[...] = inflow.astype(bf16)
    last = cum[BLOCK - 1 :, :]
    decayed = (inflow * per_head(jnp.exp(last - cum))).astype(bf16)
    state_ref[...] = state_step(state_ref[...], decayed, cum, bc_act[:, :DIM])
    total_ref[0:1, 0:HEADS] += last

    @pl.when(step == STEPS - 1)
    def _():
        for k in range(OWNERS):
            head, row = k // 16, (k % 16) * 8
            lanes = slice(head * DIM, (head + 1) * DIM)
            for r in range(8):
                payload_ref[k, :, r * 128 : (r + 1) * 128] = state_ref[row + r : row + r + 1, lanes]
            payload_ref[k, :, ASKED:] = jnp.where(
                iota((1, 128), 1) < 64, payload_ref[k, :, ASKED:], total_ref[0:1, head : head + 1]
            )


def scan_kernel(arrived_ref, before_ref):
    carried = [jnp.zeros((1, 128), f32) for _ in range(8)]
    for k in range(OWNERS):
        decay = jnp.exp(jnp.broadcast_to(arrived_ref[k, :, PAYLOAD - 1 :], (1, 128)))
        for r in range(8):
            before_ref[k, r : r + 1, :] = carried[r]
            carried[r] = carried[r] * decay + arrived_ref[k, :, r * 128 : (r + 1) * 128]


def local_kernel(
    frames_ref, normed_ref, inflow_ref, bc_ref, log_ref, z_w_ref,
    inner_ref, gate_ref, reach_ref, means_ref,
    state_ref, total_ref,
):
    @pl.when(pl.program_id(0) == 0)
    def _():
        state_ref[...] = jnp.zeros_like(state_ref)
        total_ref[...] = jnp.zeros_like(total_ref)

    gate_ref[...] = silu(dot(normed_ref[...], z_w_ref[...]).astype(bf16).astype(f32))
    pool = jnp.where(
        iota((BLOCK // 4, BLOCK), 0) == iota((BLOCK // 4, BLOCK), 1) // 4, 0.25, 0.0
    ).astype(bf16)
    means = dot(pool, frames_ref[...])
    for g in range(4):
        means_ref[g] = means[:, g * WIDTH : (g + 1) * WIDTH]
    causal = iota((BLOCK, BLOCK), 0) >= iota((BLOCK, BLOCK), 1)
    log = log_ref[:, :HEADS]
    cum = running_sum(causal, log)
    cum_rows = filled(cum).T
    b_act, c_act = bc_ref[:, :DIM], bc_ref[:, DIM:]
    inflow = inflow_ref[...]
    scores = jnp.where(causal, lax.dot_general(c_act, b_act, NT, preferred_element_type=f32), 0.0)
    carried = dot(c_act, state_ref[...].astype(bf16)) * per_head(jnp.exp(cum))
    for h in range(HEADS):
        lanes = slice(h * DIM, (h + 1) * DIM)
        gaps = jnp.minimum(cum[:, h : h + 1] - cum_rows[h : h + 1, :], 0.0)
        mixed = (jnp.exp(gaps) * scores).astype(bf16)
        inner_ref[:, lanes] = dot(mixed, inflow[:, lanes]) + carried[:, lanes]
    reach_ref[...] = filled(jnp.exp(cum + total_ref[0:1, 0:HEADS]))
    last = cum[BLOCK - 1 :, :]
    total_ref[0:1, 0:HEADS] += last
    decayed = (inflow.astype(f32) * per_head(jnp.exp(last - cum))).astype(bf16)
    state_ref[...] = state_step(state_ref[...], decayed, cum, b_act)


def outer_kernel(
    book_ref, inner_ref, gate_ref, reach_ref, c_ref, incoming_ref, gain_ref, out_w_ref,
    out_0, out_1, out_2, out_3, pooled_ref,
):
    step = pl.program_id(0)
    pool = jnp.where(
        iota((BLOCK // 4, BLOCK), 0) == iota((BLOCK // 4, BLOCK), 1) // 4, 0.25, 0.0
    ).astype(bf16)
    c_act = c_ref[...]
    for h in range(HEADS):
        lanes = slice(h * DIM, (h + 1) * DIM)
        carried = dot(c_act, incoming_ref[lanes, :].astype(bf16))
        rows = (inner_ref[:, lanes] + carried * reach_ref[:, h : h + 1]) * gate_ref[:, lanes]
        square = jnp.mean(rows * rows, axis=1, keepdims=True)
        rows = (rows * lax.rsqrt(square + 1e-05) * gain_ref[:, lanes]).astype(bf16)
        pooled_ref[pl.ds(step * (BLOCK // 4), BLOCK // 4), lanes] = dot(pool, rows)

    @pl.when(step == STEPS - 1)
    def _():
        pooled = pooled_ref[...]
        high = pooled.astype(bf16)
        low = (pooled - high.astype(f32)).astype(bf16)
        both = jnp.concatenate([high, low], axis=0)
        for shift, out in enumerate((out_0, out_1, out_2, out_3)):
            start = pl.multiple_of(((book_ref[0] + shift) % 4) * WIDTH, WIDTH)
            product = dot(both, out_w_ref[:, pl.ds(start, WIDTH)])
            out[...] = product[:QROWS] + product[QROWS:]


def split_rows(ref, values):
    rows = values.shape[0]
    ref[pl.ds(0, rows, 2), :] = values[:, :128]
    ref[pl.ds(1, rows, 2), :] = values[:, 128:]


def lookup_kernel(cuts, arrived_ref, table_ref, *refs):
    founds, (asked_ref, columns_ref, total_ref) = refs[: len(cuts)], refs[len(cuts) :]
    level = pl.program_id(0)

    @pl.when(level == 0)
    def _():
        for k in range(OWNERS):
            asked_ref[k : k + 1, :] = arrived_ref[k, :, ASKED:]
        turned = asked_ref[...].T
        start = 0
        for low, high in cuts:
            for k in range(OWNERS):
                columns_ref[start : start + high - low, :] = jnp.broadcast_to(
                    turned[low:high, k : k + 1], (high - low, 128)
                )
                start += high - low
        total_ref[...] = jnp.zeros_like(total_ref)

    place = iota((OWNERS * SLOTS, 128), 1) + (level * CODES + 1)
    asked = columns_ref[...].astype(jnp.int32)
    chosen = jnp.concatenate(
        [(asked == place + g * 128).astype(bf16) for g in range(CODES // 128)], axis=1
    )
    total_ref[...] += dot(chosen, table_ref[0].astype(bf16))

    @pl.when(level == LEVELS - 1)
    def _():
        for (low, high), found_ref in zip(cuts, founds):
            split_rows(found_ref, total_ref[OWNERS * low : OWNERS * high, :])


def joined_rows(ref):
    half = ref.shape[0] // 2
    return jnp.concatenate([ref[pl.ds(0, half, 2), :], ref[pl.ds(1, half, 2), :]], axis=1)


def pooled_kernel(
    book_ref, own_ref, from_1, from_2, from_3, means_ref, slots_ref,
    pooled_ref, base_ref, columns_ref,
):
    pooled = own_ref[...] + from_1[...] + from_2[...] + from_3[...] + means_ref[0]
    pooled_ref[...] = pooled
    slots = jnp.concatenate(
        [slots_ref[...].astype(f32), jnp.zeros((128 - LEVELS, QROWS), f32)], axis=0
    )
    columns_ref[...] = slots.T.astype(jnp.int32)
    place = iota((base_ref.shape[0], QROWS), 0)
    spread = place == slots_ref[0:1, :]
    for k in range(1, LEVELS):
        spread = spread | (place == slots_ref[k : k + 1, :])
    base_ref[...] = -folded(dot(spread.astype(bf16), two_parts(pooled)))


def residual_kernel(
    found_ref, pooled_ref, base_ref, columns_ref, slots_ref, residual_ref, grads_ref
):
    found = joined_rows(found_ref)
    rounded = found.astype(bf16)
    place = iota((QROWS, found.shape[0]), 1)
    turned = iota((found.shape[0], QROWS), 0)
    taken = jnp.zeros((QROWS, WIDTH), f32)
    terms = found + base_ref[...]
    for k in range(LEVELS):
        if k:
            spread = (turned == slots_ref[k : k + 1, :]).astype(bf16)
            terms = terms + folded(dot(spread, two_parts(taken)))
        picks = (columns_ref[:, k : k + 1] == place).astype(bf16)
        taken = taken + dot(picks, rounded)
    residual_ref[...] = pooled_ref[...] - taken
    split_rows(grads_ref, terms)


def table_kernel(codes_ref, *refs):
    grads_refs, (table_ref, rounded_ref, low_ref, high_ref) = refs[:-4], refs[-4:]
    step = pl.program_id(0)
    total = codes_ref.shape[1]

    @pl.when(step == 0)
    def _():
        start = 0
        for grads_ref in grads_refs:
            rows = grads_ref.shape[0] // 2
            rounded_ref[start : start + rows, :] = joined_rows(grads_ref).astype(bf16)
            start += rows
        code = codes_ref[...] - 1
        low_ref[...] = ((code & 127) == iota((128, total), 0)).astype(bf16)
        high_ref[...] = jnp.broadcast_to(code >> 7, (16, total))

    groups = table_ref.shape[0] // 128
    chosen = []
    for g in range(groups):
        mask = (high_ref[...] == step * groups + g).astype(bf16)
        chosen.append(low_ref[...] * jnp.concatenate([mask] * 8, axis=0))
    table_ref[...] = dot(jnp.concatenate(chosen, axis=0), rounded_ref[...])


def add_kernel(found_ref, late_ref, sum_ref):
    sum_ref[...] = found_ref[...] + late_ref[...]


def shape(*dims, dtype=f32):
    return jax.ShapeDtypeStruct(dims, dtype)


def whole(*dims):
    return pl.BlockSpec(dims, lambda *_: (0,) * len(dims))


def rows_of(rows, columns):
    return pl.BlockSpec((rows, columns), lambda i, *_: (i, 0))


def settings(mib):
    return pltpu.CompilerParams(vmem_limit_bytes=mib * 2**20)


def exchange(array):
    return lax.all_to_all(array, SEQ, split_axis=0, concat_axis=0, tiled=True)


def looked_up(arrived, codebook, cuts):
    return pl.pallas_call(
        functools.partial(lookup_kernel, cuts),
        grid=(LEVELS,),
        in_specs=[
            whole(OWNERS, 1, PAYLOAD), pl.BlockSpec((1, CODES, WIDTH), lambda i: (i, 0, 0)),
        ],
        out_specs=[whole(2 * OWNERS * (high - low), 128) for low, high in cuts],
        out_shape=[shape(2 * OWNERS * (high - low), 128) for low, high in cuts],
        scratch_shapes=[
            pltpu.VMEM((OWNERS, 128), f32), pltpu.VMEM((OWNERS * SLOTS, 128), f32),
            pltpu.VMEM((OWNERS * SLOTS, WIDTH), f32),
        ],
        compiler_params=settings(62),
        cost_estimate=pl.CostEstimate(flops=4 * 10**9, bytes_accessed=5 * 2**20, transcendentals=0),
        name="lookup",
    )(arrived, codebook)


def scanned(arrived):
    before = pl.pallas_call(
        scan_kernel,
        out_shape=shape(OWNERS, 8, 128),
        compiler_params=settings(16),
        name="scan",
    )(arrived)
    arrived, before = lax.optimization_barrier((arrived, before))
    return exchange(before).reshape(INNER, DIM), arrived


def shared_out(book, incoming, inner, gate, reach, bc_act, out_gain, out_weight):
    shares = pl.pallas_call(
        outer_kernel,
        grid_spec=pltpu.PrefetchScalarGridSpec(
            num_scalar_prefetch=1,
            grid=(STEPS,),
            in_specs=[
                rows_of(BLOCK, INNER), rows_of(BLOCK, INNER), rows_of(BLOCK, 128),
                pl.BlockSpec((BLOCK, DIM), lambda i, *_: (i, 1)),
                whole(INNER, DIM), whole(1, INNER), whole(INNER, 1024),
            ],
            out_specs=[whole(QROWS, WIDTH)] * 4,
            scratch_shapes=[pltpu.VMEM((QROWS, INNER), f32)],
        ),
        out_shape=[shape(QROWS, WIDTH)] * 4,
        compiler_params=settings(62),
        cost_estimate=pl.CostEstimate(flops=2 * 10**9, bytes_accessed=8 * 2**20, transcendentals=10**5),
        name="outer",
    )(book, inner, gate, reach, bc_act, incoming, out_gain.reshape(1, -1), out_weight)
    moved = [
        lax.ppermute(shares[d], "book", [(i, (i + d) % 4) for i in range(4)]) for d in (1, 2, 3)
    ]
    return [shares[0], *moved]


def gradient_terms(book, found, slots, shares, means):
    total = OWNERS * found.shape[1] // 2
    fetched = exchange(found)
    pooled, base, columns = pl.pallas_call(
        pooled_kernel,
        grid_spec=pltpu.PrefetchScalarGridSpec(
            num_scalar_prefetch=1,
            grid=(1,),
            in_specs=[whole(QROWS, WIDTH)] * 4
            + [
                pl.BlockSpec((1, QROWS, WIDTH), lambda i, book: (book[0], 0, 0)),
                whole(LEVELS, QROWS),
            ],
            out_specs=[
                whole(QROWS, WIDTH), whole(total, WIDTH), whole(QROWS, 128),
            ],
        ),
        out_shape=[
            shape(QROWS, WIDTH), shape(total, WIDTH), shape(QROWS, 128, dtype=jnp.int32),
        ],
        compiler_params=settings(32),
        cost_estimate=pl.CostEstimate(flops=10**9, bytes_accessed=2**20, transcendentals=0),
        name="pooled",
    )(book, *shares, means, slots)
    residual, grads = pl.pallas_call(
        residual_kernel,
        grid=(1,),
        in_specs=[
            whole(2 * total, 128), whole(QROWS, WIDTH), whole(total, WIDTH), whole(QROWS, 128),
            whole(LEVELS, QROWS),
        ],
        out_specs=[whole(QROWS, WIDTH), whole(2 * total, 128)],
        out_shape=[shape(QROWS, WIDTH), shape(2 * total, 128)],
        compiler_params=settings(24),
        cost_estimate=pl.CostEstimate(flops=10**9, bytes_accessed=2**20, transcendentals=0),
        name="residual",
    )(fetched.reshape(2 * total, 128), pooled, base, columns, slots)
    return residual, grads.reshape(found.shape)


def gathered_table(codes, *grads):
    return pl.pallas_call(
        table_kernel,
        grid=(3,),
        in_specs=[whole(*codes.shape)] + [whole(*part.shape) for part in grads],
        out_specs=rows_of(CODES, WIDTH),
        out_shape=shape(LEVELS * CODES, WIDTH),
        scratch_shapes=[
            pltpu.VMEM((codes.shape[1], WIDTH), bf16), pltpu.VMEM((128, codes.shape[1]), bf16),
            pltpu.VMEM((16, codes.shape[1]), jnp.int32),
        ],
        compiler_params=settings(40),
        name="table",
    )(codes, *grads)


def asked_codes(arrived, low, high):
    return arrived[:, 0, ASKED + low : ASKED + high].astype(jnp.int32).reshape(1, -1)


def other_core(array):
    return lax.ppermute(array, "seq_2", [(0, 1), (1, 0)])


def with_all_slots(
    book, arrived, few, slots, inner, gate, reach, means, bc_act, out_gain, out_weight, codebook
):
    incoming, arrived = scanned(arrived)
    [found] = looked_up(arrived, codebook, [(0, SLOTS)])
    shares = shared_out(book, incoming, inner, gate, reach, bc_act, out_gain, out_weight)
    residual, grads = gradient_terms(
        book, found.reshape(OWNERS, 2 * SLOTS, 128), slots, shares, means
    )
    arrived, grads = lax.optimization_barrier((arrived, grads))
    returned = exchange(grads).reshape(-1, 128)
    return residual, gathered_table(asked_codes(arrived, 0, SLOTS), returned)


def with_few_slots(
    book, arrived, few, slots, inner, gate, reach, means, bc_act, out_gain, out_weight, codebook
):
    incoming, arrived = scanned(arrived)
    found, late = looked_up(arrived, codebook, [(0, FEW), (FEW, SLOTS)])
    late = other_core(late).reshape(OWNERS, 2 * LATE, 128)
    found = found.reshape(OWNERS, 2 * FEW, 128)
    last = pl.BlockSpec((OWNERS, 2 * LATE, 128), lambda i: (0, FEW // LATE - 1, 0))
    found = pl.pallas_call(
        add_kernel,
        grid=(1,),
        in_specs=[last, whole(OWNERS, 2 * LATE, 128)],
        out_specs=last,
        out_shape=shape(OWNERS, 2 * FEW, 128),
        input_output_aliases={0: 0},
        compiler_params=settings(57),
        cost_estimate=pl.CostEstimate(flops=0, bytes_accessed=0, transcendentals=0),
        name="relayed",
    )(found, late)
    shares = shared_out(book, incoming, inner, gate, reach, bc_act, out_gain, out_weight)
    residual, grads = gradient_terms(book, found, few, shares, means)
    arrived, grads = lax.optimization_barrier((arrived, grads))
    codes = jnp.concatenate(
        [asked_codes(arrived, 0, FEW), asked_codes(arrived, FEW, SLOTS)], axis=1
    )
    returned, codes = lax.optimization_barrier((exchange(grads), codes))
    late = other_core(returned[:, 2 * (FEW - LATE) :].reshape(-1, 128))
    return residual, gathered_table(codes, returned.reshape(-1, 128), late)


def body(
    frames, norm_gain, x_weight, z_weight, bc_weight, dt_weight, dt_bias, decay_rate,
    out_gain, out_weight, codebook, code_ids,
):
    book = lax.axis_index("book").reshape(1)
    payload, slots, few, hot, normed, inflow, bc_act, log = pl.pallas_call(
        front_kernel,
        grid=(STEPS,),
        in_specs=[
            rows_of(BLOCK, 1024), whole(1, 1024), whole(1024, INNER), whole(1024, 256),
            whole(HEADS, 1024), whole(1, HEADS), whole(1, HEADS), whole(LEVELS, QROWS),
        ],
        out_specs=[
            whole(OWNERS, 1, PAYLOAD), whole(LEVELS, QROWS), whole(LEVELS, QROWS),
            whole(1, 128), rows_of(BLOCK, 1024),
            rows_of(BLOCK, INNER), rows_of(BLOCK, 256), rows_of(BLOCK, 128),
        ],
        out_shape=[
            shape(OWNERS, 1, PAYLOAD), shape(LEVELS, QROWS, dtype=jnp.int32),
            shape(LEVELS, QROWS, dtype=jnp.int32), shape(1, 128),
            shape(FRAMES, 1024, dtype=bf16), shape(FRAMES, INNER, dtype=bf16),
            shape(FRAMES, 256, dtype=bf16), shape(FRAMES, 128),
        ],
        scratch_shapes=[pltpu.VMEM((DIM, INNER), f32), pltpu.VMEM((8, 128), f32)],
        compiler_params=settings(62),
        name="front",
    )(
        frames, norm_gain.reshape(1, -1), x_weight, bc_weight, dt_weight.T,
        dt_bias.reshape(1, -1), decay_rate.reshape(1, -1), code_ids,
    )
    arrived = exchange(payload)
    inner, gate, reach, means = pl.pallas_call(
        local_kernel,
        grid=(STEPS,),
        in_specs=[
            rows_of(BLOCK, 1024), rows_of(BLOCK, 1024), rows_of(BLOCK, INNER),
            rows_of(BLOCK, 256), rows_of(BLOCK, 128), whole(1024, INNER),
        ],
        out_specs=[
            rows_of(BLOCK, INNER), rows_of(BLOCK, INNER), rows_of(BLOCK, 128),
            pl.BlockSpec((4, BLOCK // 4, WIDTH), lambda i: (0, i, 0)),
        ],
        out_shape=[
            shape(FRAMES, INNER), shape(FRAMES, INNER), shape(FRAMES, 128),
            shape(4, QROWS, WIDTH),
        ],
        scratch_shapes=[pltpu.VMEM((DIM, INNER), f32), pltpu.VMEM((8, 128), f32)],
        compiler_params=settings(62),
        cost_estimate=pl.CostEstimate(flops=4 * 10**9, bytes_accessed=12 * 2**20, transcendentals=10**6),
        name="local",
    )(frames, normed, inflow, bc_act, log, z_weight)
    arrived, inner = lax.optimization_barrier((arrived, inner))
    residual, table = lax.cond(
        hot[0, 0] < 1.5, with_few_slots, with_all_slots,
        book, arrived, few, slots, inner, gate, reach, means, bc_act, out_gain, out_weight, codebook,
    )
    return residual, table.reshape(LEVELS, CODES, WIDTH)


def solution(mesh):
    finer = Mesh(
        mesh.devices.reshape(8, 4, 2, mesh.shape["book"]), ("seq_0", "seq_1", "seq_2", "book")
    )
    placed = (
        P(SEQ, None), P(), P(None, "book"), P(None, "book"), P(), P(None, "book"), P("book"),
        P("book"), P("book"), P("book", None), P(None, SEQ, "book"), P(None, SEQ),
    )
    return jax.shard_map(
        body,
        mesh=finer,
        in_specs=placed,
        out_specs=(P(SEQ, "book"), P(None, SEQ, "book")),
        check_vma=False,
    )
```
